256 devices in a mesh: expert: 64 (over y, z, core), etp: 4 (over x).
Axes of the slice: x: 4, y: 4, z: 8, core: 2. Of those that a mesh axis runs over, the one named last changes fastest.
Arguments:
- grad_out: bfloat16 [32768, 7168], P(('expert', 'etp')), may hold values from -1.5 to 1.5
- grad_exponent: int32 [32768, 56], P(('expert', 'etp')), may hold values from -2 to 1
- expert_ids: int32 [32768, 2], P(('expert', 'etp')), may hold values from 0 to 63, all different within a row; in each aligned block of 128 rows (0 to 127, 128 to 255, ...) at most 6 rows name the same one
- combine: bfloat16 [32768, 2], P(('expert', 'etp')), may hold values from 0.099609375 to 1
- saved_acts: bfloat16 [64, 4, 64, 6, 2, 1024], P('expert', 'etp'), may hold values from -6 to 6
- w_down: bfloat16 [64, 1024, 7168], P('expert', None, 'etp'), may hold values from -0.1875 to 0.1875
Outputs:
- pre_grad: bfloat16 [64, 4, 64, 6, 2, 1024], P('expert', 'etp')
- grad_down: bfloat16 [64, 1024, 7168], P('expert', None, 'etp')
- router_grad: float32 [32768, 2], P(('expert', 'etp'))
The draws below stay inside these ranges and needn't reach their ends.
Inputs may be any that keep to these rules, and one draw needn't show every extreme that they name: `expert_ids`: in the rows of one device each expert is named at most 6 times, a bound that some block reaches; a token names 2 different experts.
All inputs are finite; a program needn't handle non-finite values.
Results may differ from the reference program's by a relative error of at most 0.0049.
Values may be sent and summed in bfloat16 or wider, within the bound.
A program may use at most 128 MiB of HBM per device.

```python
import math
import jax
import jax.numpy as jnp
import numpy as np
from jax import lax

D = 7168
FF = 1024
TOK_DEV = 128
TOP = 2
QB = 128
EXPERTS = 64
CAP = 6
TOKENS = 32768
N_EXPERT = 64
N_ETP = 4


def place_ends(values, rng, low, high):
    longest = values.shape.index(max(values.shape))
    spots = []
    for shift in (0, 1):
        where = [jax.random.randint(jax.random.fold_in(rng, axis), (), 0, length) for axis, length in enumerate(values.shape)]
        where[longest] = (where[longest] + shift) % values.shape[longest]
        spots.append(tuple(where))
    return values.at[spots[0]].set(low).at[spots[1]].set(high)


def steps_of(own_key, shape, cuts, least, largest):
    factor_of = 1.0
    for axis_at, shards_of in cuts:
        draws = jax.random.uniform(jax.random.fold_in(jax.random.fold_in(own_key, 6), axis_at), (shards_of,), jnp.float32, least / len(cuts), largest / len(cuts))
        factor_of = factor_of * jnp.repeat(jnp.exp(draws), shape[axis_at] // shards_of).reshape((-1,) + (1,) * (len(shape) - 1 - axis_at))
    return factor_of


def deal_out(rng, own, number, rows, count, top, reach, slope):
    ranking = jax.random.permutation(rng, count)
    heavy_load, usual = portions_of(count, rows * top, reach, slope, True), portions_of(count, rows * top, reach, slope, False)
    places = jnp.arange(count)

    def named(lengths, offset_by):
        used = int((lengths > 0).sum())
        fixed = max(1, used // 4)
        passed = fixed + (places - fixed + offset_by * (used - fixed)) % max(1, count - fixed)
        return jnp.zeros((count,), jnp.int32).at[ranking[jnp.where(places < fixed, places, passed)]].set(jnp.asarray(lengths, jnp.int32))

    lengths = jnp.where(number % 4 == 0, named(heavy_load, number // 4), named(usual, number - number // 4 - 1))
    mixed = jax.random.permutation(jax.random.fold_in(own, 3), count)
    giver, taker = mixed[0:count // 2 * 2:2], mixed[1:count // 2 * 2:2]
    slack = jnp.minimum(lengths[giver] - 1, reach - lengths[taker]) // 2
    slack = jnp.where((giver == ranking[0]) | (taker == ranking[0]) | (lengths[taker] == 0), 0, jnp.maximum(slack, 0))
    passed = jax.random.randint(jax.random.fold_in(own, 4), (count // 2,), 0, 1 << 20) % (slack + 1)
    lengths = lengths.at[giver].add(-passed).at[taker].add(passed)
    items = jnp.searchsorted(jnp.cumsum(lengths), jnp.arange(rows * top), side="right").astype(jnp.int32)
    grid = items.reshape(top, rows).T
    grid = grid[jax.random.permutation(jax.random.fold_in(own, 1), rows)]
    offset_by = jax.random.randint(jax.random.fold_in(own, 2), (rows, 1), 0, top)
    return jnp.take_along_axis(grid, (jnp.arange(top)[None, :] + offset_by) % top, axis=1)


def portions_of(number_of, total, reach, lean, full):
    portions = [(1 << 20) // math.isqrt(standing ** lean) + 1 for standing in range(1, number_of + 1)]
    largest = reach if full else min(reach, max(-(-total // number_of), total * portions[0] // sum(portions)))
    least = 1 if total - largest >= number_of - 1 else 0
    given, rest = [largest] + [least] * (number_of - 1), total - largest - least * (number_of - 1)
    while rest > 0:
        free = [i for i in range(1, number_of) if given[i] < largest] or [i for i in range(1, number_of) if given[i] < reach]
        whole, budget = sum([portions[i] for i in free]), rest
        for i in free:
            more = min(reach - given[i], max(1, budget * portions[i] // whole), rest)
            given[i] = given[i] + more
            rest = rest - more
    return np.array(given)


def noise(rng, shape, deviation, limit, shards=(), kind=jnp.bfloat16):
    result = jax.random.normal(rng, shape, jnp.float32) * deviation
    if len(shards) > 0:
        result = steps_of(rng, shape, shards, -0.22, 0.18) * result
    return jnp.clip(result, min=-limit, max=limit).astype(kind)


def setup_inputs(seed: int = 0) -> dict:
    splits = jax.random.split(jax.random.key(seed), 7)
    grad_out = noise(splits[0], (TOKENS, D), 0.25, 1.5, ((0, 256),))
    grad_exponent = place_ends(jax.random.randint(splits[1], (TOKENS, D // QB), -2, 2), jax.random.fold_in(splits[1], 1), -2, 1).astype(jnp.int32)
    expert_ids_keys = jax.random.split(jax.random.fold_in(splits[2], 1), TOKENS // TOK_DEV)
    expert_ids_turns = jax.random.permutation(jax.random.fold_in(splits[2], 3), TOKENS // TOK_DEV)
    expert_ids = jax.vmap(lambda own, number: deal_out(jax.random.fold_in(splits[2], 2), own, number, TOK_DEV, EXPERTS, TOP, CAP, 1))(expert_ids_keys, expert_ids_turns).reshape((TOKENS, TOP))
    combine = jnp.clip(jnp.exp(math.log(1.0) - 2.306499 * jax.random.uniform(splits[3], (TOKENS, TOP), jnp.float32) ** steps_of(splits[3], (TOKENS, TOP), ((0, 256),), -0.2, 0.2)), 0.099609375, 1.0).astype(jnp.bfloat16)
    saved_acts = noise(splits[4], (EXPERTS, N_ETP, N_EXPERT, CAP, 2, FF), 1.0, 6.0, ((0, 64), (1, 4)))
    w_down = noise(splits[5], (EXPERTS, FF, D), FF ** -0.5, 0.1875, ((0, 64), (2, 4)))
    return dict(grad_out=grad_out, grad_exponent=grad_exponent, expert_ids=expert_ids, combine=combine, saved_acts=saved_acts, w_down=w_down)


def power_of_two(exponent):
    return jnp.where(exponent <= -2, 0.25, jnp.where(exponent == -1, 0.5, jnp.where(exponent == 0, 1.0, 2.0))).astype(jnp.float32)


def backward_local(raw_grad, saved_rows, weight_rows):
    gate_pre = saved_rows[:, 0, :].astype(jnp.float32)
    up_pre = saved_rows[:, 1, :].astype(jnp.float32)
    sigmoid_gate = jax.nn.sigmoid(gate_pre)
    silu_gate = gate_pre * sigmoid_gate
    hidden = silu_gate * up_pre
    router_part = jnp.sum(hidden * raw_grad, axis=1)
    hidden_grad = weight_rows[:, None] * raw_grad
    grad_gate = hidden_grad * up_pre * (sigmoid_gate * (1.0 + gate_pre * (1.0 - sigmoid_gate)))
    grad_up = hidden_grad * silu_gate
    pre_grad = jnp.stack([grad_gate, grad_up], axis=1).astype(jnp.bfloat16)
    scaled = (weight_rows[:, None] * hidden).astype(jnp.bfloat16)
    return pre_grad, scaled, router_part


def reference(grad_out, grad_exponent, expert_ids, combine, saved_acts, w_down):
    device_count = N_EXPERT * N_ETP
    row_dev = TOK_DEV * TOP
    block_scale = power_of_two(grad_exponent)
    dequant = (grad_out.astype(jnp.float32).reshape(TOKENS, D // QB, QB) * block_scale[:, :, None]).reshape(TOKENS, D).astype(jnp.bfloat16)
    route_ids = expert_ids.reshape(device_count, row_dev)
    onehot = (route_ids[:, :, None] == jnp.arange(EXPERTS, dtype=jnp.int32)[None, None, :]).astype(jnp.int32)
    earlier = jnp.cumsum(onehot, axis=1) - onehot
    slot_index = jnp.sum(earlier * onehot, axis=2)
    device = jnp.arange(device_count, dtype=jnp.int32)[:, None]
    position = ((route_ids * N_ETP + device % N_ETP) * N_EXPERT + device // N_ETP) * CAP + slot_index
    global_row = device * row_dev + jnp.arange(row_dev, dtype=jnp.int32)[None, :]
    slot_total = N_ETP * N_EXPERT * CAP
    table = jnp.full((EXPERTS * slot_total,), -1, jnp.int32).at[position.reshape(-1)].set(global_row.reshape(-1)).reshape(EXPERTS, slot_total)
    flat_weights = combine.reshape(-1)

    def per_expert(inputs):
        source_row, saved, weight = inputs
        filled = source_row >= 0
        safe_row = jnp.maximum(source_row, 0)
        row_data = jnp.where(filled[:, None], dequant[safe_row // TOP], jnp.zeros((), jnp.bfloat16))
        weight_rows = jnp.where(filled, flat_weights[safe_row], jnp.zeros((), jnp.bfloat16)).astype(jnp.float32)
        raw_grad = jnp.dot(row_data, weight.T, preferred_element_type=jnp.float32)
        pre_grad, scaled, router_part = backward_local(raw_grad, saved.reshape(slot_total, 2, FF), weight_rows)
        grad_total = jnp.dot(scaled.T, row_data, preferred_element_type=jnp.float32).astype(jnp.bfloat16)
        return pre_grad, grad_total, router_part

    pre_grad, grad_down, router_slot = lax.map(per_expert, (table, saved_acts, w_down))
    sink = jnp.where(table >= 0, table, TOKENS * TOP)
    router_grad = jnp.zeros((TOKENS * TOP,), jnp.float32).at[sink.reshape(-1)].set(router_slot.reshape(-1), mode="drop")
    return pre_grad.reshape(saved_acts.shape), grad_down, router_grad.reshape(TOKENS, TOP)
```

```python
import functools

import jax
import jax.numpy as jnp
import numpy as np
from jax import lax
from jax.experimental import pallas as pl
from jax.experimental.pallas import tpu as pltpu
from jax.sharding import PartitionSpec as P

MESH = pl.DeviceIdType.MESH
F32, BF16, I32 = jnp.float32, jnp.bfloat16, jnp.int32
NY, NZ, NC = 4, 8, 2
HALVES = 2


def power_of_two(exponent):
    return jnp.where(
        exponent <= -2, 0.25, jnp.where(exponent == -1, 0.5, jnp.where(exponent == 0, 1.0, 2.0))
    ).astype(F32)


def matmul(a, b):
    return jnp.dot(a, b, preferred_element_type=F32)


def constants(nx, cap, tok):
    gs = NY * NC
    rc = nx * cap
    own = gs * cap
    order = np.zeros((HALVES, gs * rc, gs * HALVES * rc), np.float32)
    for h in range(HALVES):
        for r in range(nx):
            for i in range(gs):
                for c in range(cap):
                    order[h, r * own + i * cap + c, (i * HALVES + h) * rc + r * cap + c] = 1
    split = np.zeros((2 * own, 2 * own), np.float32)
    for g in range(2):
        for j in range(own):
            split[g * own + j, 2 * j + g] = 1
    repeat = np.zeros((own, gs), np.float32)
    for j in range(own):
        repeat[j, j // cap] = 1
    pick = np.zeros((own, 128), np.float32)
    diag = np.zeros((own, 128), np.float32)
    for j in range(own):
        pick[j, j % cap] = 1
        diag[j, j] = 1
    before = np.triu(np.ones((tok, tok), np.float32), 1)
    bf = lambda a: jnp.asarray(a, BF16)
    return bf(order), bf(split), bf(split.T), bf(repeat), jnp.asarray(pick), jnp.asarray(diag), bf(before)


def kernel(
    nx, cap,
    grad_ref, exp_ref, ids_ref, comb_ref, saved_hbm, w_hbm,
    order_ref, split_ref, join_ref, repeat_ref, pick_ref, diag_ref, before_ref,
    pre_hbm, down_hbm, router_ref,
    xs, tok, ksend, krecv, keys, sbuf, rbuf, rows, w, sv, pstage, wsend, wrecv, wcol,
    scaled, scaled_all, scaled_t, pf, psend, precv, rrow, rrecv, down,
    in_sem, x_ssem, x_rsem, k_ssem, k_rsem, d_ssem, d_rsem, d_lsem, w_ssem, w_rsem,
    g_ssem, g_rsem, g_lsem, p_ssem, p_rsem, r_ssem, r_rsem, o_sem, o2_sem,
):
    me = lax.axis_index("expert")
    q = lax.axis_index("etp")
    y, z, core = me // (NZ * NC), (me // NC) % NZ, me % NC
    gs = NY * NC
    rc = nx * cap
    mr = HALVES * rc
    own = gs * cap
    ne = NY * NZ * NC
    tokens = grad_ref.shape[0]
    width = w.shape[1]
    half = width // HALVES
    blocks = exp_ref.shape[0]
    inner = [(dy, dc) for dy in range(NY) for dc in range(NC)]
    slot_me = y * NC + core

    def expert_of(dy, dz, dc):
        return ((y + dy) % NY) * (NZ * NC) + ((z + dz) % NZ) * NC + (core + dc) % NC

    def remote(src, dst, ssem, rsem, e, x):
        return pltpu.make_async_remote_copy(
            src_ref=src, dst_ref=dst, send_sem=ssem, recv_sem=rsem, device_id=(e, x), device_id_type=MESH
        )

    def plane_order(g):
        d = (g + 1) // 2
        return (NZ // 2 + d * (1 - 2 * (g % 2)) * -1 + NZ) % NZ

    w_in = pltpu.make_async_copy(w_hbm, w, in_sem.at[0])
    w_in.start()
    s_in = [pltpu.make_async_copy(saved_hbm.at[:, j], sv.at[j], in_sem.at[1 + j]) for j in range(NZ)]
    for c in s_in:
        c.start()

    bar = pltpu.get_barrier_semaphore()
    for d in range(1, nx):
        pl.semaphore_signal(bar, inc=1, device_id=(me, (q + d) % nx), device_id_type=MESH)

    def greet(k, _):
        pl.semaphore_signal(bar, inc=1, device_id=((me + k) % ne, q), device_id_type=MESH)
        return 0

    lax.fori_loop(1, ne, greet, 0)

    expert_iota = lax.broadcasted_iota(I32, (ne, tokens), 0)
    a = [jnp.where(expert_iota == ids_ref[k : k + 1, :], 1.0, 0.0) for k in range(2)]
    assigned = a[0] + a[1]
    slot = matmul(assigned.astype(BF16), before_ref[...])
    slot = jnp.where(assigned > 0, slot, -1.0)
    ksend[...] = slot
    combine = comb_ref[...].astype(F32)
    weight = a[0] * combine[0:1, :] + a[1] * combine[1:2, :]
    lane = lax.broadcasted_iota(I32, (ne, 128), 1)
    slot_weight = jnp.zeros((ne, 128), F32)
    for c in range(cap):
        total = jnp.sum(jnp.where(slot == c, weight, 0.0), axis=1, keepdims=True)
        slot_weight = jnp.where(lane == c, total, slot_weight)
    wsend[...] = slot_weight.reshape(ne, 1, 128)

    scale_t = power_of_two(exp_ref[...]).astype(BF16)
    blk = width // (width * nx // blocks)
    qb = width // blk
    block_iota = lax.broadcasted_iota(I32, (blocks, width), 0)
    col_block = lax.broadcasted_iota(I32, (blocks, width), 1) // qb
    for j in range(nx):
        expand = jnp.where(block_iota == col_block + j * blk, 1.0, 0.0).astype(BF16)
        scale = lax.dot_general(scale_t, expand, (((0,), (0,)), ((), ())), preferred_element_type=F32)
        deq = (grad_ref[:, j * width : (j + 1) * width].astype(F32) * scale).astype(BF16)
        for h in range(HALVES):
            xs[j, h] = deq[:, h * half : (h + 1) * half]

    pl.semaphore_wait(bar, ne - 1 + nx - 1)

    k_out, x_out = [], []
    for d in range(1, nx):
        p = (q + d) % nx
        k_out.append(remote(ksend, krecv.at[q], k_ssem.at[d - 1], k_rsem, me, p))
        k_out[-1].start()
    for d in range(1, nx):
        p = (q + d) % nx
        x_out.append(remote(xs.at[p], tok.at[:, q], x_ssem.at[d - 1], x_rsem, me, p))
        x_out[-1].start()
    x_own = pltpu.make_async_copy(xs.at[q], tok.at[:, q], in_sem.at[NZ + 1])
    x_own.start()
    krecv[q] = ksend[...]

    def send_weight(k, _):
        dz, rest = k // gs, k % gs
        dy, dc = rest // NC, rest % NC
        e = expert_of(dy, dz, dc)
        remote(wsend.at[e], wrecv.at[dz * gs + slot_me], w_ssem, w_rsem, e, q).start()
        return 0

    lax.fori_loop(1, ne, send_weight, 0)
    wrecv[slot_me] = wsend[me]

    remote(krecv.at[pl.ds(0, nx - 1)], krecv.at[pl.ds(0, nx - 1)], k_ssem.at[0], k_rsem, me, (q + 1) % nx).wait_recv()
    for r in range(nx):
        s = krecv[r]
        for h in range(HALVES):
            at = (h * nx + r) * tokens
            keys[:, at : at + tokens] = jnp.where(s >= 0, s + (h * rc + r * cap), -1.0)

    remote(tok.at[:, pl.ds(0, nx - 1)], tok.at[:, pl.ds(0, nx - 1)], x_ssem.at[0], x_rsem, me, (q + 1) % nx).wait_recv()
    x_own.wait()

    row_iota = lax.broadcasted_iota(I32, (mr, HALVES * nx * tokens), 0).astype(F32)

    def dispatch(g, _):
        dz = plane_order(g)
        for i in range(gs):
            e = (i // NC) * (NZ * NC) + ((z + dz) % NZ) * NC + i % NC
            hot = jnp.where(row_iota == keys[pl.ds(e, 1), :], 1.0, 0.0).astype(BF16)
            out = matmul(hot, tok[...].reshape(HALVES * nx * tokens, half))
            sbuf[dz, i * mr : (i + 1) * mr, :] = out.astype(BF16)

        def send(dy, dc):
            to = ((y + dy) % NY) * NC + (core + dc) % NC
            remote(
                sbuf.at[dz, pl.ds(pl.multiple_of(to * mr, mr), mr)],
                rbuf.at[dz, pl.ds(pl.multiple_of(slot_me * mr, mr), mr)],
                d_ssem.at[dz], d_rsem.at[dz], expert_of(dy, dz, dc), q,
            ).start()

        for dy, dc in inner:
            if (dy, dc) == (0, 0):
                @pl.when(dz != 0)
                def _():
                    send(0, 0)

                @pl.when(dz == 0)
                def _():
                    pltpu.make_async_copy(
                        sbuf.at[dz, pl.ds(pl.multiple_of(slot_me * mr, mr), mr)],
                        rbuf.at[dz, pl.ds(pl.multiple_of(slot_me * mr, mr), mr)],
                        d_lsem,
                    ).start()
            else:
                send(dy, dc)
        return 0

    lax.fori_loop(0, NZ, dispatch, 0)

    for c in s_in:
        c.wait()
    remote(wrecv.at[pl.ds(0, ne - 1)], wrecv.at[pl.ds(0, ne - 1)], w_ssem, w_rsem, me, (q + 1) % nx).wait_recv()

    def gate_up(dz):
        v = sv[(z - dz + NZ) % NZ].reshape(2 * own, w.shape[0])
        gu = matmul(split_ref[...], v)
        gate, up = gu[:own], gu[own:]
        sg = jax.nn.sigmoid(gate)
        return gate, up, sg, gate * sg

    def scale_hidden(dz, _):
        gate, up, sg, silu = gate_up(dz)
        wr = wrecv[pl.ds(dz * gs, gs)].reshape(gs, 128)
        col = jnp.sum(matmul(repeat_ref[...], wr.astype(BF16)) * pick_ref[...], axis=1, keepdims=True)
        wcol[dz] = jnp.broadcast_to(col, (own, 128))
        scaled[dz] = (col * (silu * up)).astype(BF16)
        return 0

    lax.fori_loop(0, NZ, scale_hidden, 0)
    g_out = []
    for d in range(1, nx):
        g_out.append(remote(scaled, scaled_all.at[:, q], g_ssem.at[d - 1], g_rsem, me, (q + d) % nx))
        g_out[-1].start()
    g_own = pltpu.make_async_copy(scaled, scaled_all.at[:, q], g_lsem)
    g_own.start()
    w_in.wait()
    remote(scaled_all.at[:, pl.ds(0, nx - 1)], scaled_all.at[:, pl.ds(0, nx - 1)], g_ssem.at[0], g_rsem, me, (q + 1) % nx).wait_recv()
    g_own.wait()
    ff = w.shape[0]
    flat_scaled = scaled_all.reshape(NZ * nx * own, ff)
    step = 256

    def turn(k, _):
        at = pl.multiple_of(k * step, step)
        scaled_t[:, pl.ds(at, step)] = flat_scaled[pl.ds(at, step), :].T
        return 0

    lax.fori_loop(0, NZ * nx * own // step, turn, 0)

    grp = nx * own

    def finish(g):
        dz = plane_order(g)
        zz = (z - dz + NZ) % NZ
        remote(precv.at[dz, pl.ds(0, nx - 1)], precv.at[dz, pl.ds(0, nx - 1)], p_ssem.at[dz], p_rsem.at[dz], me, (q + 1) % nx).wait_recv()
        raw = pf[g % 2, pl.ds(pl.multiple_of(q * own, own), own), :]
        for d in range(1, nx):
            raw = raw + precv[dz, (q + d) % nx].astype(F32)
        gate, up, sg, silu = gate_up(dz)
        part = jnp.sum(silu * up * raw, axis=1, keepdims=True)
        rrow[dz] = jnp.sum(part * diag_ref[...], axis=0, keepdims=True)
        for dy, dc in inner:
            e = (((y + dy) % NY) * NZ + zz) * NC + (core + dc) % NC

            def send():
                remote(rrow.at[dz], rrecv.at[me], r_ssem, r_rsem, e, q).start()

            if (dy, dc) == (0, 0):
                pl.when(dz != 0)(send)

                @pl.when(dz == 0)
                def _():
                    rrecv[me] = rrow[dz]
            else:
                send()
        hg = wcol[dz][:, 0:1] * raw
        g_gate = hg * up * (sg * (1.0 + gate * (1.0 - sg)))
        g_up = hg * silu
        both = jnp.concatenate([g_gate, g_up], axis=0).astype(BF16)
        pstage[zz] = matmul(join_ref[...], both).astype(BF16).reshape(pstage.shape[1:])
        pltpu.make_async_copy(pstage.at[zz], pre_hbm.at[:, zz], o_sem.at[zz]).start()

    def arrive(g, _):
        dz = plane_order(g)

        @pl.when(dz != 0)
        def _():
            remote(rbuf.at[dz], rbuf.at[dz], d_ssem.at[dz], d_rsem.at[dz], me, (q + 1) % nx).wait_recv()

        @pl.when(dz == 0)
        def _():
            part = rbuf.at[dz, pl.ds(0, (gs - 1) * mr)]
            remote(part, part, d_ssem.at[dz], d_rsem.at[dz], me, (q + 1) % nx).wait_recv()
            block = rbuf.at[dz, pl.ds(pl.multiple_of(slot_me * mr, mr), mr)]
            pltpu.make_async_copy(block, block, d_lsem).wait()

        at = pl.multiple_of(dz * grp, grp)
        for h in range(HALVES):
            rows[pl.ds(at, grp), h * half : (h + 1) * half] = matmul(order_ref[h], rbuf[dz]).astype(BF16)
        part = lax.dot_general(
            rows[pl.ds(at, grp), :], w[...], (((1,), (1,)), ((), ())), preferred_element_type=F32
        )
        pf[g % 2] = part
        psend[dz] = part.astype(BF16)
        for d in range(1, nx):
            p = (q + d) % nx
            remote(
                psend.at[dz, pl.ds(pl.multiple_of(p * own, own), own)], precv.at[dz, q],
                p_ssem.at[dz], p_rsem.at[dz], me, p,
            ).start()

        @pl.when(g > 0)
        def _():
            finish(g - 1)

        return 0

    lax.fori_loop(0, NZ, arrive, 0)

    def down_tile(k, _):
        at = pl.multiple_of(k * step, step)
        down[:, pl.ds(at, step)] = matmul(scaled_t[...], rows[:, pl.ds(at, step)]).astype(BF16)
        pltpu.make_async_copy(down.at[:, pl.ds(at, step)], down_hbm.at[:, pl.ds(at, step)], o2_sem.at[k]).start()
        return 0

    lax.fori_loop(0, width // step, down_tile, 0)
    finish(NZ - 1)

    remote(rrecv.at[pl.ds(0, ne - 1)], rrecv.at[pl.ds(0, ne - 1)], r_ssem, r_rsem, me, (q + 1) % nx).wait_recv()
    back = rrecv[...].reshape(ne, 128)
    value = jnp.zeros((ne, tokens), F32)
    for c in range(cap):
        column = jnp.sum(jnp.where(lane == slot_me * cap + c, back, 0.0), axis=1, keepdims=True)
        value = jnp.where(ksend[...] == c, column, value)
    for k in range(2):
        mine = jnp.where(expert_iota == ids_ref[k : k + 1, :], value, 0.0)
        router_ref[k : k + 1, :] = jnp.sum(mine, axis=0, keepdims=True)

    for c in k_out + x_out + g_out:
        c.wait_send()
    part = wsend.at[pl.ds(0, ne - 1)]
    remote(part, part, w_ssem, w_rsem, me, (q + 1) % nx).wait_send()
    part = rrecv.at[pl.ds(0, ne - 1)]
    remote(part, part, r_ssem, r_rsem, me, (q + 1) % nx).wait_send()
    for j in range(NZ):
        part = sbuf.at[j] if j else sbuf.at[j, pl.ds(0, (gs - 1) * mr)]
        remote(part, part, d_ssem.at[j], d_rsem.at[j], me, (q + 1) % nx).wait_send()
        part = psend.at[j, pl.ds(0, (nx - 1) * own)]
        remote(part, part, p_ssem.at[j], p_rsem.at[j], me, (q + 1) % nx).wait_send()
        pltpu.make_async_copy(pstage.at[j], pre_hbm.at[:, j], o_sem.at[j]).wait()
    for k in range(width // step):
        pltpu.make_async_copy(
            down.at[:, k * step : (k + 1) * step], down_hbm.at[:, k * step : (k + 1) * step], o2_sem.at[k]
        ).wait()


def local(grad_out, grad_exponent, expert_ids, combine, saved_acts, w_down):
    nx = lax.axis_size("etp")
    ne = NY * NZ * NC
    tokens, features = grad_out.shape
    cap, ff = saved_acts.shape[3], saved_acts.shape[5]
    width = features // nx
    half = width // HALVES
    gs = NY * NC
    own = gs * cap
    mr = HALVES * nx * cap
    consts = constants(nx, cap, tokens)
    vmem = pl.BlockSpec(memory_space=pltpu.VMEM)
    hbm = pl.BlockSpec(memory_space=pl.ANY)
    dma = pltpu.SemaphoreType.DMA
    saved = saved_acts.reshape(NY, NZ, NC * cap, 2, ff)
    pre, down, router = pl.pallas_call(
        functools.partial(kernel, nx, cap),
        out_shape=[
            jax.ShapeDtypeStruct(saved.shape, BF16),
            jax.ShapeDtypeStruct((ff, width), BF16),
            jax.ShapeDtypeStruct((2, tokens), F32),
        ],
        in_specs=[vmem] * 4 + [hbm] * 2 + [vmem] * len(consts),
        out_specs=[hbm, hbm, vmem],
        scratch_shapes=[
            pltpu.VMEM((nx, HALVES, tokens, half), BF16),
            pltpu.VMEM((HALVES, nx, tokens, half), BF16),
            pltpu.VMEM((ne, tokens), F32),
            pltpu.VMEM((nx, ne, tokens), F32),
            pltpu.VMEM((ne, HALVES * nx * tokens), F32),
            pltpu.VMEM((NZ, gs * mr, half), BF16),
            pltpu.VMEM((NZ, gs * mr, half), BF16),
            pltpu.VMEM((NZ * nx * own, width), BF16),
            pltpu.VMEM((ff, width), BF16),
            pltpu.VMEM((NZ, NY, NC * cap, 2, ff), BF16),
            pltpu.VMEM((NZ, NY, NC * cap, 2, ff), BF16),
            pltpu.VMEM((ne, 1, 128), F32),
            pltpu.VMEM((ne, 1, 128), F32),
            pltpu.VMEM((NZ, own, 128), F32),
            pltpu.VMEM((NZ, own, ff), BF16),
            pltpu.VMEM((NZ, nx, own, ff), BF16),
            pltpu.VMEM((ff, NZ * nx * own), BF16),
            pltpu.VMEM((2, nx * own, ff), F32),
            pltpu.VMEM((NZ, nx * own, ff), BF16),
            pltpu.VMEM((NZ, nx, own, ff), BF16),
            pltpu.VMEM((NZ, 1, 128), F32),
            pltpu.VMEM((ne, 1, 128), F32),
            pltpu.VMEM((ff, width), BF16),
            dma((NZ + 2,)),
            dma((nx - 1,)), dma,
            dma((nx - 1,)), dma,
            dma((NZ,)), dma((NZ,)), dma,
            dma, dma,
            dma((nx - 1,)), dma, dma,
            dma((NZ,)), dma((NZ,)),
            dma, dma,
            dma((NZ,)), dma((width // 256,)),
        ],
        compiler_params=pltpu.CompilerParams(
            collective_id=0, has_side_effects=True, vmem_limit_bytes=60 << 20
        ),
    )(grad_out, grad_exponent.T, expert_ids.T, combine.T, saved, w_down[0], *consts)
    return pre.reshape(saved_acts.shape), down[None], router.T


def solution(mesh):
    placed = (
        P(("expert", "etp"), None),
        P(("expert", "etp"), None),
        P(("expert", "etp"), None),
        P(("expert", "etp"), None),
        P("expert", "etp", None, None, None, None),
        P("expert", None, "etp"),
    )
    return jax.shard_map(
        local,
        mesh=mesh,
        in_specs=placed,
        out_specs=(
            P("expert", "etp", None, None, None, None),
            P("expert", None, "etp"),
            P(("expert", "etp"), None),
        ),
        check_vma=False,
    )
```

```python
import functools

import jax
import jax.numpy as jnp
import numpy as np
from jax import lax
from jax.experimental import pallas as pl
from jax.experimental.pallas import tpu as pltpu
from jax.sharding import PartitionSpec as P

MESH = pl.DeviceIdType.MESH
F32, BF16, I32 = jnp.float32, jnp.bfloat16, jnp.int32
NY, NZ, NC = 4, 8, 2
HALVES = 2
EARLY = 256


def power_of_two(exponent):
    return jnp.where(
        exponent <= -2, 0.25, jnp.where(exponent == -1, 0.5, jnp.where(exponent == 0, 1.0, 2.0))
    ).astype(F32)


def matmul(a, b):
    return jnp.dot(a, b, preferred_element_type=F32)


def constants(nx, cap, tok):
    gs = NY * NC
    rc = nx * cap
    own = gs * cap
    order = np.zeros((HALVES, gs * rc, gs * HALVES * rc), np.float32)
    for h in range(HALVES):
        for r in range(nx):
            for i in range(gs):
                for c in range(cap):
                    order[h, r * own + i * cap + c, (i * HALVES + h) * rc + r * cap + c] = 1
    split = np.zeros((2 * own, 2 * own), np.float32)
    for g in range(2):
        for j in range(own):
            split[g * own + j, 2 * j + g] = 1
    repeat = np.zeros((own, gs), np.float32)
    for j in range(own):
        repeat[j, j // cap] = 1
    pick = np.zeros((own, 128), np.float32)
    diag = np.zeros((own, 128), np.float32)
    for j in range(own):
        pick[j, j % cap] = 1
        diag[j, j] = 1
    before = np.triu(np.ones((tok, tok), np.float32), 1)
    bf = lambda a: jnp.asarray(a, BF16)
    return bf(order), bf(split), bf(split.T), bf(repeat), jnp.asarray(pick), jnp.asarray(diag), bf(before)


def kernel(
    nx, cap,
    grad_ref, exp_ref, ids_ref, comb_ref, saved_hbm, w_hbm,
    order_ref, split_ref, join_ref, repeat_ref, pick_ref, diag_ref, before_ref,
    pre_hbm, down_hbm, router_ref,
    xs, tok, ksend, krecv, keys, sbuf, rbuf, rows, w, sv, pstage, wsend, wrecv, wcol,
    scaled, scaled_all, scaled_t, pf, psend, precv, rrow, rrecv, acc, down,
    in_sem, x_ssem, x_rsem, k_ssem, k_rsem, d_ssem, d_rsem, d_lsem, w_ssem, w_rsem,
    g_ssem, g_rsem, g_lsem, p_ssem, p_rsem, r_ssem, r_rsem, o_sem, o2_sem,
):
    me = lax.axis_index("expert")
    q = lax.axis_index("etp")
    y, z, core = me // (NZ * NC), (me // NC) % NZ, me % NC
    gs = NY * NC
    rc = nx * cap
    mr = HALVES * rc
    own = gs * cap
    ne = NY * NZ * NC
    tokens = grad_ref.shape[0]
    width = w.shape[1]
    half = width // HALVES
    blocks = exp_ref.shape[0]
    inner = [(dy, dc) for dy in range(NY) for dc in range(NC)]
    slot_me = y * NC + core

    def expert_of(dy, dz, dc):
        return ((y + dy) % NY) * (NZ * NC) + ((z + dz) % NZ) * NC + (core + dc) % NC

    def remote(src, dst, ssem, rsem, e, x):
        return pltpu.make_async_remote_copy(
            src_ref=src, dst_ref=dst, send_sem=ssem, recv_sem=rsem, device_id=(e, x), device_id_type=MESH
        )

    def far_first(g):
        return (NZ // 2 + ((g + 1) // 2) * (2 * (g % 2) - 1) + NZ) % NZ

    def own_first(g):
        return (NZ // 2 * ((g + NZ - 1) // NZ) + (g // 2) * (1 - 2 * (g % 2)) + NZ) % NZ

    w_in = pltpu.make_async_copy(w_hbm, w, in_sem.at[0])
    w_in.start()
    s_in = [pltpu.make_async_copy(saved_hbm.at[:, j], sv.at[j], in_sem.at[1 + j]) for j in range(NZ)]
    for c in s_in:
        c.start()

    bar = pltpu.get_barrier_semaphore()
    for d in range(1, nx):
        pl.semaphore_signal(bar, inc=1, device_id=(me, (q + d) % nx), device_id_type=MESH)

    def greet(k, _):
        pl.semaphore_signal(bar, inc=1, device_id=((me + k) % ne, q), device_id_type=MESH)
        return 0

    lax.fori_loop(1, ne, greet, 0)

    expert_iota = lax.broadcasted_iota(I32, (ne, tokens), 0)
    a = [jnp.where(expert_iota == ids_ref[k : k + 1, :], 1.0, 0.0) for k in range(2)]
    assigned = a[0] + a[1]
    slot = matmul(assigned.astype(BF16), before_ref[...])
    slot = jnp.where(assigned > 0, slot, -1.0)
    ksend[...] = slot
    combine = comb_ref[...].astype(F32)
    weight = a[0] * combine[0:1, :] + a[1] * combine[1:2, :]
    lane = lax.broadcasted_iota(I32, (ne, 128), 1)
    slot_weight = jnp.zeros((ne, 128), F32)
    for c in range(cap):
        total = jnp.sum(jnp.where(slot == c, weight, 0.0), axis=1, keepdims=True)
        slot_weight = jnp.where(lane == c, total, slot_weight)
    wsend[...] = slot_weight.reshape(ne, 1, 128)

    scale_t = power_of_two(exp_ref[...]).astype(BF16)
    blk = width // (width * nx // blocks)
    qb = width // blk
    block_iota = lax.broadcasted_iota(I32, (blocks, width), 0)
    col_block = lax.broadcasted_iota(I32, (blocks, width), 1) // qb
    for j in range(nx):
        expand = jnp.where(block_iota == col_block + j * blk, 1.0, 0.0).astype(BF16)
        scale = lax.dot_general(scale_t, expand, (((0,), (0,)), ((), ())), preferred_element_type=F32)
        deq = (grad_ref[:, j * width : (j + 1) * width].astype(F32) * scale).astype(BF16)
        for h in range(HALVES):
            xs[j, h] = deq[:, h * half : (h + 1) * half]

    pl.semaphore_wait(bar, ne - 1 + nx - 1)

    k_out, x_out = [], []
    for d in range(1, nx):
        p = (q + d) % nx
        k_out.append(remote(ksend, krecv.at[q], k_ssem.at[d - 1], k_rsem, me, p))
        k_out[-1].start()
    cuts = [slice(0, EARLY), slice(EARLY, half)]
    for part, cut in enumerate(cuts):
        for d in range(1, nx):
            p = (q + d) % nx
            x_out.append(
                remote(xs.at[p, :, :, cut], tok.at[:, q, :, cut], x_ssem.at[part, d - 1], x_rsem.at[part], me, p)
            )
            x_out[-1].start()
    x_own = pltpu.make_async_copy(xs.at[q], tok.at[:, q], in_sem.at[NZ + 1])
    x_own.start()
    krecv[q] = ksend[...]

    def send_weight(k, _):
        dz, rest = k // gs, k % gs
        dy, dc = rest // NC, rest % NC
        e = expert_of(dy, dz, dc)
        remote(wsend.at[e], wrecv.at[dz * gs + slot_me], w_ssem, w_rsem, e, q).start()
        return 0

    lax.fori_loop(1, ne, send_weight, 0)
    wrecv[slot_me] = wsend[me]

    remote(krecv.at[pl.ds(0, nx - 1)], krecv.at[pl.ds(0, nx - 1)], k_ssem.at[0], k_rsem, me, (q + 1) % nx).wait_recv()
    for r in range(nx):
        s = krecv[r]
        for h in range(HALVES):
            at = (h * nx + r) * tokens
            keys[:, at : at + tokens] = jnp.where(s >= 0, s + (h * rc + r * cap), -1.0)

    x_own.wait()

    row_iota = lax.broadcasted_iota(I32, (mr, HALVES * nx * tokens), 0).astype(F32)

    def dispatch(part, order, g, _):
        cut = cuts[part]
        dz = order(g)
        for i in range(gs):
            e = (i // NC) * (NZ * NC) + ((z + dz) % NZ) * NC + i % NC
            hot = jnp.where(row_iota == keys[pl.ds(e, 1), :], 1.0, 0.0).astype(BF16)
            out = matmul(hot, tok[:, :, :, cut].reshape(HALVES * nx * tokens, cut.stop - cut.start))
            sbuf[dz, i * mr : (i + 1) * mr, cut] = out.astype(BF16)

        mine = pl.ds(pl.multiple_of(slot_me * mr, mr), mr)

        def send(dy, dc):
            to = ((y + dy) % NY) * NC + (core + dc) % NC
            remote(
                sbuf.at[dz, pl.ds(pl.multiple_of(to * mr, mr), mr), cut], rbuf.at[dz, mine, cut],
                d_ssem.at[dz], d_rsem.at[dz], expert_of(dy, dz, dc), q,
            ).start()

        for dy, dc in inner:
            if (dy, dc) == (0, 0):
                @pl.when(dz != 0)
                def _():
                    send(0, 0)

                @pl.when(dz == 0)
                def _():
                    pltpu.make_async_copy(sbuf.at[dz, mine, cut], rbuf.at[dz, mine, cut], d_lsem).start()
            else:
                send(dy, dc)
        return 0

    for part, order in enumerate((far_first, own_first)):
        cut = cuts[part]
        landed = tok.at[:, pl.ds(0, nx - 1), :, cut]
        remote(landed, landed, x_ssem.at[part, 0], x_rsem.at[part], me, (q + 1) % nx).wait_recv()
        lax.fori_loop(0, NZ, functools.partial(dispatch, part, order), 0)

    for c in s_in:
        c.wait()
    remote(wrecv.at[pl.ds(0, ne - 1)], wrecv.at[pl.ds(0, ne - 1)], w_ssem, w_rsem, me, (q + 1) % nx).wait_recv()

    def gate_up(dz):
        v = sv[(z - dz + NZ) % NZ].reshape(2 * own, w.shape[0])
        gu = matmul(split_ref[...], v)
        gate, up = gu[:own], gu[own:]
        sg = jax.nn.sigmoid(gate)
        return gate, up, sg, gate * sg

    def scale_hidden(g, _):
        dz = own_first(g)
        gate, up, sg, silu = gate_up(dz)
        wr = wrecv[pl.ds(dz * gs, gs)].reshape(gs, 128)
        col = jnp.sum(matmul(repeat_ref[...], wr.astype(BF16)) * pick_ref[...], axis=1, keepdims=True)
        wcol[g] = jnp.broadcast_to(col, (own, 128))
        scaled[g] = (col * (silu * up)).astype(BF16)
        return 0

    lax.fori_loop(0, NZ, scale_hidden, 0)
    g_out = []
    for d in range(1, nx):
        g_out.append(remote(scaled, scaled_all.at[:, q], g_ssem.at[d - 1], g_rsem, me, (q + d) % nx))
        g_out[-1].start()
    g_own = pltpu.make_async_copy(scaled, scaled_all.at[:, q], g_lsem)
    g_own.start()
    w_in.wait()

    ff = w.shape[0]
    step = 256

    def turn_scaled():
        remote(scaled_all.at[:, pl.ds(0, nx - 1)], scaled_all.at[:, pl.ds(0, nx - 1)], g_ssem.at[0], g_rsem, me, (q + 1) % nx).wait_recv()
        g_own.wait()
        flat_scaled = scaled_all.reshape(NZ * nx * own, ff)

        def turn(k, _):
            at = pl.multiple_of(k * step, step)
            scaled_t[:, pl.ds(at, step)] = flat_scaled[pl.ds(at, step), :].T
            return 0

        lax.fori_loop(0, NZ * nx * own // step, turn, 0)

    grp = nx * own
    planes = [own_first(g) for g in range(NZ)]

    def finish(g):
        dz = planes[g]
        zz = (z - dz + NZ) % NZ
        landed = precv.at[dz, pl.ds(0, nx - 1)]
        remote(landed, landed, p_ssem.at[dz], p_rsem.at[dz], me, (q + 1) % nx).wait_recv()
        raw = pf[g % 2, pl.ds(pl.multiple_of(q * own, own), own), :]
        for d in range(1, nx):
            raw = raw + precv[dz, (q + d) % nx].astype(F32)
        gate, up, sg, silu = gate_up(dz)
        part = jnp.sum(silu * up * raw, axis=1, keepdims=True)
        rrow[dz] = jnp.sum(part * diag_ref[...], axis=0, keepdims=True)
        for dy, dc in inner:
            e = (((y + dy) % NY) * NZ + zz) * NC + (core + dc) % NC

            def send():
                remote(rrow.at[dz], rrecv.at[me], r_ssem, r_rsem, e, q).start()

            if (dy, dz, dc) == (0, 0, 0):
                rrecv[me] = rrow[dz]
            else:
                send()
        hg = wcol[g][:, 0:1] * raw
        g_gate = hg * up * (sg * (1.0 + gate * (1.0 - sg)))
        g_up = hg * silu
        both = jnp.concatenate([g_gate, g_up], axis=0).astype(BF16)
        pstage[zz] = matmul(join_ref[...], both).astype(BF16).reshape(pstage.shape[1:])
        pltpu.make_async_copy(pstage.at[zz], pre_hbm.at[:, zz], o_sem.at[zz]).start()

    def arrive(g):
        dz = planes[g]
        if dz:
            remote(rbuf.at[dz], rbuf.at[dz], d_ssem.at[dz], d_rsem.at[dz], me, (q + 1) % nx).wait_recv()
        else:
            part = rbuf.at[dz, pl.ds(0, (gs - 1) * mr)]
            remote(part, part, d_ssem.at[dz], d_rsem.at[dz], me, (q + 1) % nx).wait_recv()
            block = rbuf.at[dz, pl.ds(pl.multiple_of(slot_me * mr, mr), mr)]
            pltpu.make_async_copy(block, block, d_lsem).wait()
        at = g * grp
        for h in range(HALVES):
            rows[at : at + grp, h * half : (h + 1) * half] = matmul(order_ref[h], rbuf[dz]).astype(BF16)
        part = lax.dot_general(
            rows[at : at + grp, :], w[...], (((1,), (1,)), ((), ())), preferred_element_type=F32
        )
        pf[g % 2] = part
        psend[dz] = part.astype(BF16)
        for d in range(1, nx):
            p = (q + d) % nx
            remote(
                psend.at[dz, pl.ds(pl.multiple_of(p * own, own), own)], precv.at[dz, q],
                p_ssem.at[dz], p_rsem.at[dz], me, p,
            ).start()

    def product(lo, hi, first, last):
        def tile(k, _):
            at = pl.ds(pl.multiple_of(k * step, step), step)
            total = matmul(scaled_t[:, lo * grp : hi * grp], rows[lo * grp : hi * grp, at])
            if not first:
                total = total + acc[:, at]
            if last:
                down[:, at] = total.astype(BF16)
                pltpu.make_async_copy(down.at[:, at], down_hbm.at[:, at], o2_sem.at[k]).start()
            else:
                acc[:, at] = total
            return 0

        lax.fori_loop(0, width // step, tile, 0)

    arrive(0)
    arrive(1)
    turn_scaled()
    finish(0)
    finish(1)
    arrive(2)
    arrive(3)
    product(0, 4, True, False)
    finish(2)
    finish(3)
    arrive(4)
    arrive(5)
    product(4, 6, False, False)
    finish(4)
    finish(5)
    arrive(6)
    arrive(7)
    product(6, 8, False, True)
    finish(6)
    finish(7)

    remote(rrecv.at[pl.ds(0, ne - 1)], rrecv.at[pl.ds(0, ne - 1)], r_ssem, r_rsem, me, (q + 1) % nx).wait_recv()
    back = rrecv[...].reshape(ne, 128)
    value = jnp.zeros((ne, tokens), F32)
    for c in range(cap):
        column = jnp.sum(jnp.where(lane == slot_me * cap + c, back, 0.0), axis=1, keepdims=True)
        value = jnp.where(ksend[...] == c, column, value)
    for k in range(2):
        mine = jnp.where(expert_iota == ids_ref[k : k + 1, :], value, 0.0)
        router_ref[k : k + 1, :] = jnp.sum(mine, axis=0, keepdims=True)

    for c in k_out + x_out + g_out:
        c.wait_send()
    part = wsend.at[pl.ds(0, ne - 1)]
    remote(part, part, w_ssem, w_rsem, me, (q + 1) % nx).wait_send()
    part = rrecv.at[pl.ds(0, ne - 1)]
    remote(part, part, r_ssem, r_rsem, me, (q + 1) % nx).wait_send()
    for j in range(NZ):
        part = sbuf.at[j] if j else sbuf.at[j, pl.ds(0, (gs - 1) * mr)]
        remote(part, part, d_ssem.at[j], d_rsem.at[j], me, (q + 1) % nx).wait_send()
        part = psend.at[j, pl.ds(0, (nx - 1) * own)]
        remote(part, part, p_ssem.at[j], p_rsem.at[j], me, (q + 1) % nx).wait_send()
        pltpu.make_async_copy(pstage.at[j], pre_hbm.at[:, j], o_sem.at[j]).wait()
    for k in range(width // step):
        pltpu.make_async_copy(
            down.at[:, k * step : (k + 1) * step], down_hbm.at[:, k * step : (k + 1) * step], o2_sem.at[k]
        ).wait()


def local(grad_out, grad_exponent, expert_ids, combine, saved_acts, w_down):
    nx = lax.axis_size("etp")
    ne = NY * NZ * NC
    tokens, features = grad_out.shape
    cap, ff = saved_acts.shape[3], saved_acts.shape[5]
    width = features // nx
    half = width // HALVES
    gs = NY * NC
    own = gs * cap
    mr = HALVES * nx * cap
    consts = constants(nx, cap, tokens)
    vmem = pl.BlockSpec(memory_space=pltpu.VMEM)
    hbm = pl.BlockSpec(memory_space=pl.ANY)
    dma = pltpu.SemaphoreType.DMA
    saved = saved_acts.reshape(NY, NZ, NC * cap, 2, ff)
    pre, down, router = pl.pallas_call(
        functools.partial(kernel, nx, cap),
        out_shape=[
            jax.ShapeDtypeStruct(saved.shape, BF16),
            jax.ShapeDtypeStruct((ff, width), BF16),
            jax.ShapeDtypeStruct((2, tokens), F32),
        ],
        in_specs=[vmem] * 4 + [hbm] * 2 + [vmem] * len(consts),
        out_specs=[hbm, hbm, vmem],
        scratch_shapes=[
            pltpu.VMEM((nx, HALVES, tokens, half), BF16),
            pltpu.VMEM((HALVES, nx, tokens, half), BF16),
            pltpu.VMEM((ne, tokens), F32),
            pltpu.VMEM((nx, ne, tokens), F32),
            pltpu.VMEM((ne, HALVES * nx * tokens), F32),
            pltpu.VMEM((NZ, gs * mr, half), BF16),
            pltpu.VMEM((NZ, gs * mr, half), BF16),
            pltpu.VMEM((NZ * nx * own, width), BF16),
            pltpu.VMEM((ff, width), BF16),
            pltpu.VMEM((NZ, NY, NC * cap, 2, ff), BF16),
            pltpu.VMEM((NZ, NY, NC * cap, 2, ff), BF16),
            pltpu.VMEM((ne, 1, 128), F32),
            pltpu.VMEM((ne, 1, 128), F32),
            pltpu.VMEM((NZ, own, 128), F32),
            pltpu.VMEM((NZ, own, ff), BF16),
            pltpu.VMEM((NZ, nx, own, ff), BF16),
            pltpu.VMEM((ff, NZ * nx * own), BF16),
            pltpu.VMEM((2, nx * own, ff), F32),
            pltpu.VMEM((NZ, nx * own, ff), BF16),
            pltpu.VMEM((NZ, nx, own, ff), BF16),
            pltpu.VMEM((NZ, 1, 128), F32),
            pltpu.VMEM((ne, 1, 128), F32),
            pltpu.VMEM((ff, width), F32),
            pltpu.VMEM((ff, width), BF16),
            dma((NZ + 2,)),
            dma((2, nx - 1)), dma((2,)),
            dma((nx - 1,)), dma,
            dma((NZ,)), dma((NZ,)), dma,
            dma, dma,
            dma((nx - 1,)), dma, dma,
            dma((NZ,)), dma((NZ,)),
            dma, dma,
            dma((NZ,)), dma((width // 256,)),
        ],
        compiler_params=pltpu.CompilerParams(
            collective_id=0, has_side_effects=True, vmem_limit_bytes=60 << 20
        ),
    )(grad_out, grad_exponent.T, expert_ids.T, combine.T, saved, w_down[0], *consts)
    return pre.reshape(saved_acts.shape), down[None], router.T


def solution(mesh):
    placed = (
        P(("expert", "etp"), None),
        P(("expert", "etp"), None),
        P(("expert", "etp"), None),
        P(("expert", "etp"), None),
        P("expert", "etp", None, None, None, None),
        P("expert", None, "etp"),
    )
    return jax.shard_map(
        local,
        mesh=mesh,
        in_specs=placed,
        out_specs=(
            P("expert", "etp", None, None, None, None),
            P("expert", None, "etp"),
            P(("expert", "etp"), None),
        ),
        check_vma=False,
    )
```

```python
import functools

import jax
import jax.numpy as jnp
import numpy as np
from jax import lax
from jax.experimental import pallas as pl
from jax.experimental.pallas import tpu as pltpu
from jax.sharding import PartitionSpec as P

MESH = pl.DeviceIdType.MESH
F32, BF16, I32 = jnp.float32, jnp.bfloat16, jnp.int32
NY, NZ, NC = 4, 8, 2
HALVES = 2
CUTS = (0, 128, 384)


def power_of_two(exponent):
    return jnp.where(
        exponent <= -2, 0.25, jnp.where(exponent == -1, 0.5, jnp.where(exponent == 0, 1.0, 2.0))
    ).astype(F32)


def matmul(a, b):
    return jnp.dot(a, b, preferred_element_type=F32)


def constants(nx, cap, tok):
    gs = NY * NC
    rc = nx * cap
    own = gs * cap
    order = np.zeros((HALVES, gs * rc, gs * HALVES * rc), np.float32)
    for h in range(HALVES):
        for r in range(nx):
            for i in range(gs):
                for c in range(cap):
                    order[h, r * own + i * cap + c, (i * HALVES + h) * rc + r * cap + c] = 1
    split = np.zeros((2 * own, 2 * own), np.float32)
    for g in range(2):
        for j in range(own):
            split[g * own + j, 2 * j + g] = 1
    repeat = np.zeros((own, gs), np.float32)
    for j in range(own):
        repeat[j, j // cap] = 1
    pick = np.zeros((own, 128), np.float32)
    diag = np.zeros((own, 128), np.float32)
    for j in range(own):
        pick[j, j % cap] = 1
        diag[j, j] = 1
    before = np.triu(np.ones((tok, tok), np.float32), 1)
    bf = lambda a: jnp.asarray(a, BF16)
    return bf(order), bf(split), bf(split.T), bf(repeat), jnp.asarray(pick), jnp.asarray(diag), bf(before)


def kernel(
    nx, cap,
    grad_ref, exp_ref, ids_ref, comb_ref, saved_hbm, w_hbm,
    order_ref, split_ref, join_ref, repeat_ref, pick_ref, diag_ref, before_ref,
    pre_hbm, down_hbm, router_ref,
    xs, tok, ksend, krecv, keys, sbuf, rbuf, rows, w, sv, pstage, wsend, wrecv, wcol,
    scaled, scaled_all, scaled_t, pf, psend, precv, rrow, rrecv, acc, down,
    in_sem, x_ssem, x_rsem, k_ssem, k_rsem, d_ssem, d_rsem, d_lsem, w_ssem, w_rsem,
    g_ssem, g_rsem, g_lsem, p_ssem, p_rsem, r_ssem, r_rsem, o_sem, o2_sem,
):
    me = lax.axis_index("expert")
    q = lax.axis_index("etp")
    y, z, core = me // (NZ * NC), (me // NC) % NZ, me % NC
    gs = NY * NC
    rc = nx * cap
    mr = HALVES * rc
    own = gs * cap
    ne = NY * NZ * NC
    tokens = grad_ref.shape[0]
    width = w.shape[1]
    half = width // HALVES
    blocks = exp_ref.shape[0]

    def expert_of(dy, dz, dc):
        return ((y + dy) % NY) * (NZ * NC) + ((z + dz) % NZ) * NC + (core + dc) % NC

    def remote(src, dst, ssem, rsem, e, x):
        return pltpu.make_async_remote_copy(
            src_ref=src, dst_ref=dst, send_sem=ssem, recv_sem=rsem, device_id=(e, x), device_id_type=MESH
        )

    def step_of(k, j):
        paired = (k + NZ - 2) // NZ
        far = (1 + ((k + NZ - 2) % NZ) // 2) * (1 - 2 * (j // 2))
        dz = (1 - paired) * (NZ // 2) * k + paired * (NZ // 2 + far)
        dy = (1 - paired) * j + paired * (2 * (k % 2) + j % 2)
        return dy, (dz + NZ) % NZ

    def source(k, j):
        dy, dz = step_of(k, j)
        return (y - dy + NY) % NY, (z - dz + NZ) % NZ

    w_in = pltpu.make_async_copy(w_hbm, w, in_sem.at[0])
    w_in.start()

    def load_saved(n, _):
        sy, sz = source(n // NY, n % NY)
        pltpu.make_async_copy(saved_hbm.at[sy, sz], sv.at[n // NY, n % NY], in_sem.at[1]).start()
        return 0


    bar = pltpu.get_barrier_semaphore()
    for d in range(1, nx):
        pl.semaphore_signal(bar, inc=1, device_id=(me, (q + d) % nx), device_id_type=MESH)

    def greet(k, _):
        pl.semaphore_signal(bar, inc=1, device_id=((me + k) % ne, q), device_id_type=MESH)
        return 0

    lax.fori_loop(1, ne, greet, 0)

    expert_iota = lax.broadcasted_iota(I32, (ne, tokens), 0)
    a = [jnp.where(expert_iota == ids_ref[k : k + 1, :], 1.0, 0.0) for k in range(2)]
    assigned = a[0] + a[1]
    slot = matmul(assigned.astype(BF16), before_ref[...])
    slot = jnp.where(assigned > 0, slot, -1.0)
    ksend[...] = slot.astype(BF16)
    combine = comb_ref[...].astype(F32)
    weight = a[0] * combine[0:1, :] + a[1] * combine[1:2, :]
    lane = lax.broadcasted_iota(I32, (ne, 128), 1)
    slot_weight = jnp.zeros((ne, 128), F32)
    for c in range(cap):
        total = jnp.sum(jnp.where(slot == c, weight, 0.0), axis=1, keepdims=True)
        slot_weight = jnp.where(lane == c, total, slot_weight)
    wsend[...] = slot_weight.reshape(ne, 1, 128)

    scale_t = power_of_two(exp_ref[...]).astype(BF16)
    blk = width // (width * nx // blocks)
    qb = width // blk
    block_iota = lax.broadcasted_iota(I32, (blocks, width), 0)
    col_block = lax.broadcasted_iota(I32, (blocks, width), 1) // qb
    for j in range(nx):
        expand = jnp.where(block_iota == col_block + j * blk, 1.0, 0.0).astype(BF16)
        scale = lax.dot_general(scale_t, expand, (((0,), (0,)), ((), ())), preferred_element_type=F32)
        deq = (grad_ref[:, j * width : (j + 1) * width].astype(F32) * scale).astype(BF16)
        for h in range(HALVES):
            xs[j, h] = deq[:, h * half : (h + 1) * half]

    pl.semaphore_wait(bar, ne - 1 + nx - 1)

    k_out, x_out = [], []
    for d in range(1, nx):
        p = (q + d) % nx
        k_out.append(remote(ksend, krecv.at[q], k_ssem.at[d - 1], k_rsem, me, p))
        k_out[-1].start()
    cuts = [slice(lo, hi) for lo, hi in zip(CUTS, CUTS[1:] + (half,))]
    for part, cut in enumerate(cuts):
        for d in range(1, nx):
            p = (q + d) % nx
            x_out.append(
                remote(xs.at[p, :, :, cut], tok.at[:, q, :, cut], x_ssem.at[part, d - 1], x_rsem.at[part], me, p)
            )
            x_out[-1].start()
    x_own = pltpu.make_async_copy(xs.at[q], tok.at[:, q], in_sem.at[2])
    x_own.start()
    krecv[q] = ksend[...]
    lax.fori_loop(0, NZ * NY, load_saved, 0)

    def send_weight(k, _):
        group, j, dc = k // gs, (k % gs) // NC, k % NC
        dy, dz = step_of(group, j)
        e = expert_of(dy, dz, dc)
        remote(wsend.at[e], wrecv.at[group * gs + j * NC + core], w_ssem, w_rsem, e, q).start()
        return 0


    remote(krecv.at[pl.ds(0, nx - 1)], krecv.at[pl.ds(0, nx - 1)], k_ssem.at[0], k_rsem, me, (q + 1) % nx).wait_recv()
    for r in range(nx):
        s = krecv[r].astype(F32)
        for h in range(HALVES):
            at = (h * nx + r) * tokens
            keys[:, at : at + tokens] = jnp.where(s >= 0, s + (h * rc + r * cap), -1.0)

    x_own.wait()

    row_iota = lax.broadcasted_iota(I32, (mr, HALVES * nx * tokens), 0).astype(F32)

    own_block = pl.ds(pl.multiple_of(core * mr, mr), mr)

    def dispatch(part, turn, g, _):
        cut = cuts[part]
        k = (g + turn) % NZ
        for j in range(NY):
            dy, dz = step_of(k, j)
            for c in range(NC):
                e = (((y + dy) % NY) * NZ + (z + dz) % NZ) * NC + c
                hot = jnp.where(row_iota == keys[pl.ds(e, 1), :], 1.0, 0.0).astype(BF16)
                out = matmul(hot, tok[:, :, :, cut].reshape(HALVES * nx * tokens, cut.stop - cut.start))
                i = j * NC + c
                sbuf[k, i * mr : (i + 1) * mr, cut] = out.astype(BF16)

        def send(j, dc):
            dy, dz = step_of(k, j)
            to = j * NC + (core + dc) % NC
            at = j * NC + core
            remote(
                sbuf.at[k, pl.ds(pl.multiple_of(to * mr, mr), mr), cut],
                rbuf.at[k, pl.ds(pl.multiple_of(at * mr, mr), mr), cut],
                d_ssem.at[k], d_rsem.at[k], expert_of(dy, dz, dc), q,
            ).start()

        for j in range(NY):
            for dc in range(NC):
                if (j, dc) == (0, 0):
                    @pl.when(k != 0)
                    def _():
                        send(0, 0)

                    @pl.when(k == 0)
                    def _():
                        pltpu.make_async_copy(sbuf.at[k, own_block, cut], rbuf.at[k, own_block, cut], d_lsem).start()
                else:
                    send(j, dc)
        return 0

    for part, cut in enumerate(cuts):
        landed = tok.at[:, pl.ds(0, nx - 1), :, cut]
        remote(landed, landed, x_ssem.at[part, 0], x_rsem.at[part], me, (q + 1) % nx).wait_recv()
        lax.fori_loop(0, NZ, functools.partial(dispatch, part, 0 if part == len(cuts) - 1 else 1), 0)
        if part == 0:
            lax.fori_loop(1, ne, send_weight, 0)
            wrecv[core] = wsend[me]

    pltpu.make_async_copy(sv, sv, in_sem.at[1]).wait()
    remote(wrecv.at[pl.ds(0, ne - 1)], wrecv.at[pl.ds(0, ne - 1)], w_ssem, w_rsem, me, (q + 1) % nx).wait_recv()

    def gate_up(k):
        v = sv[k].reshape(2 * own, w.shape[0])
        gu = matmul(split_ref[...], v)
        gate, up = gu[:own], gu[own:]
        sg = jax.nn.sigmoid(gate)
        return gate, up, sg, gate * sg

    def scale_hidden(g, _):
        gate, up, sg, silu = gate_up(g)
        wr = wrecv[pl.ds(g * gs, gs)].reshape(gs, 128)
        col = jnp.sum(matmul(repeat_ref[...], wr.astype(BF16)) * pick_ref[...], axis=1, keepdims=True)
        wcol[g] = jnp.broadcast_to(col, (own, 128))
        scaled[g] = (col * (silu * up)).astype(BF16)
        return 0

    lax.fori_loop(0, NZ, scale_hidden, 0)
    g_out = []
    for d in range(1, nx):
        g_out.append(remote(scaled, scaled_all.at[:, q], g_ssem.at[d - 1], g_rsem, me, (q + d) % nx))
        g_out[-1].start()
    g_own = pltpu.make_async_copy(scaled, scaled_all.at[:, q], g_lsem)
    g_own.start()
    w_in.wait()

    ff = w.shape[0]
    step = 256

    def turn_scaled():
        remote(scaled_all.at[:, pl.ds(0, nx - 1)], scaled_all.at[:, pl.ds(0, nx - 1)], g_ssem.at[0], g_rsem, me, (q + 1) % nx).wait_recv()
        g_own.wait()
        flat_scaled = scaled_all.reshape(NZ * nx * own, ff)

        def turn(k, _):
            at = pl.multiple_of(k * step, step)
            scaled_t[:, pl.ds(at, step)] = flat_scaled[pl.ds(at, step), :].T
            return 0

        lax.fori_loop(0, NZ * nx * own // step, turn, 0)

    grp = nx * own

    def finish(g):
        landed = precv.at[g, pl.ds(0, nx - 1)]
        remote(landed, landed, p_ssem.at[g], p_rsem.at[g], me, (q + 1) % nx).wait_recv()
        raw = pf[g % 2, pl.ds(pl.multiple_of(q * own, own), own), :]
        for d in range(1, nx):
            raw = raw + precv[g, (q + d) % nx].astype(F32)
        gate, up, sg, silu = gate_up(g)
        part = jnp.sum(silu * up * raw, axis=1, keepdims=True)
        rrow[g] = jnp.sum(part * diag_ref[...], axis=0, keepdims=True)
        for j in range(NY):
            sy, sz = source(g, j)
            for dc in range(NC):
                if (g, j, dc) == (0, 0, 0):
                    rrecv[me] = rrow[g]
                else:
                    e = (sy * NZ + sz) * NC + (core + dc) % NC
                    remote(rrow.at[g], rrecv.at[me], r_ssem, r_rsem, e, q).start()
        hg = wcol[g][:, 0:1] * raw
        g_gate = hg * up * (sg * (1.0 + gate * (1.0 - sg)))
        g_up = hg * silu
        both = jnp.concatenate([g_gate, g_up], axis=0).astype(BF16)
        pstage[g] = matmul(join_ref[...], both).astype(BF16).reshape(pstage.shape[1:])
        for j in range(NY):
            sy, sz = source(g, j)
            pltpu.make_async_copy(pstage.at[g, j], pre_hbm.at[sy, sz], o_sem.at[g]).start()

    def arrive(g):
        if g:
            remote(rbuf.at[g], rbuf.at[g], d_ssem.at[g], d_rsem.at[g], me, (q + 1) % nx).wait_recv()
        else:
            part = rbuf.at[g, pl.ds(0, (gs - 1) * mr)]
            remote(part, part, d_ssem.at[g], d_rsem.at[g], me, (q + 1) % nx).wait_recv()
            block = rbuf.at[g, own_block]
            pltpu.make_async_copy(block, block, d_lsem).wait()
        at = g * grp
        for h in range(HALVES):
            rows[at : at + grp, h * half : (h + 1) * half] = matmul(order_ref[h], rbuf[g]).astype(BF16)
        part = lax.dot_general(
            rows[at : at + grp, :], w[...], (((1,), (1,)), ((), ())), preferred_element_type=F32
        )
        pf[g % 2] = part
        psend[g] = part.astype(BF16)
        for d in range(1, nx):
            p = (q + d) % nx
            remote(
                psend.at[g, pl.ds(pl.multiple_of(p * own, own), own)], precv.at[g, q],
                p_ssem.at[g], p_rsem.at[g], me, p,
            ).start()

    def product(lo, hi, first, last):
        def tile(k, _):
            at = pl.ds(pl.multiple_of(k * step, step), step)
            total = matmul(scaled_t[:, lo * grp : hi * grp], rows[lo * grp : hi * grp, at])
            if not first:
                total = total + acc[:, at]
            if last:
                down[:, at] = total.astype(BF16)
                pltpu.make_async_copy(down.at[:, at], down_hbm.at[:, at], o2_sem.at[k]).start()
            else:
                acc[:, at] = total
            return 0

        lax.fori_loop(0, width // step, tile, 0)

    arrive(0)
    arrive(1)
    turn_scaled()
    finish(0)
    arrive(2)
    finish(1)
    arrive(3)
    product(0, 4, True, False)
    finish(2)
    arrive(4)
    finish(3)
    arrive(5)
    product(4, 6, False, False)
    finish(4)
    arrive(6)
    finish(5)
    arrive(7)
    finish(6)
    product(6, 8, False, True)
    finish(7)

    remote(rrecv.at[pl.ds(0, ne - 1)], rrecv.at[pl.ds(0, ne - 1)], r_ssem, r_rsem, me, (q + 1) % nx).wait_recv()
    back = rrecv[...].reshape(ne, 128)
    value = jnp.zeros((ne, tokens), F32)
    slot = ksend[...].astype(F32)
    expert = lax.broadcasted_iota(I32, (ne, 128), 0)
    dy = (expert // (NZ * NC) - y + NY) % NY
    dz = ((expert // NC) % NZ - z + NZ) % NZ
    j = jnp.where(dz % (NZ // 2) == 0, dy, dy % 2 + jnp.where(dz < NZ // 2, 2, 0))
    place = (j * NC + core) * cap
    for c in range(cap):
        column = jnp.sum(jnp.where(lane == place + c, back, 0.0), axis=1, keepdims=True)
        value = jnp.where(slot == c, column, value)
    for k in range(2):
        mine = jnp.where(expert_iota == ids_ref[k : k + 1, :], value, 0.0)
        router_ref[k : k + 1, :] = jnp.sum(mine, axis=0, keepdims=True)

    for c in k_out + x_out + g_out:
        c.wait_send()
    part = wsend.at[pl.ds(0, ne - 1)]
    remote(part, part, w_ssem, w_rsem, me, (q + 1) % nx).wait_send()
    part = rrecv.at[pl.ds(0, ne - 1)]
    remote(part, part, r_ssem, r_rsem, me, (q + 1) % nx).wait_send()
    for j in range(NZ):
        part = sbuf.at[j] if j else sbuf.at[j, pl.ds(0, (gs - 1) * mr)]
        remote(part, part, d_ssem.at[j], d_rsem.at[j], me, (q + 1) % nx).wait_send()
        part = psend.at[j, pl.ds(0, (nx - 1) * own)]
        remote(part, part, p_ssem.at[j], p_rsem.at[j], me, (q + 1) % nx).wait_send()
        pltpu.make_async_copy(pstage.at[j], pre_hbm.at[:, j], o_sem.at[j]).wait()
    for k in range(width // step):
        pltpu.make_async_copy(
            down.at[:, k * step : (k + 1) * step], down_hbm.at[:, k * step : (k + 1) * step], o2_sem.at[k]
        ).wait()


def hand_over(pieces, pre_in, down_in, router_in, pre_out, down_out, router_out, pre_buf, down_buf, in_sem, out_sem):
    parts = []
    rows = down_buf.shape[0] // pieces
    for j in range(pieces):
        at = pl.ds(j * rows, rows)
        parts.append((down_in.at[at], down_buf.at[at], down_out.at[at]))
    for j in range(pre_buf.shape[0]):
        for i in range(pre_buf.shape[1]):
            parts.append((pre_in.at[j, i], pre_buf.at[j, i], pre_out.at[j, i]))
    loads = [pltpu.make_async_copy(a, b, in_sem.at[n]) for n, (a, b, _) in enumerate(parts)]
    stores = [pltpu.make_async_copy(b, c, out_sem.at[n]) for n, (_, b, c) in enumerate(parts)]
    for c in loads:
        c.start()
    router_out[...] = router_in[...]
    for load, store in zip(loads, stores):
        load.wait()
        store.start()
    for c in stores:
        c.wait()


def local(grad_out, grad_exponent, expert_ids, combine, saved_acts, w_down):
    nx = lax.axis_size("etp")
    ne = NY * NZ * NC
    tokens, features = grad_out.shape
    cap, ff = saved_acts.shape[3], saved_acts.shape[5]
    width = features // nx
    half = width // HALVES
    gs = NY * NC
    own = gs * cap
    mr = HALVES * nx * cap
    consts = constants(nx, cap, tokens)
    vmem = pl.BlockSpec(memory_space=pltpu.VMEM)
    hbm = pl.BlockSpec(memory_space=pl.ANY)
    dma = pltpu.SemaphoreType.DMA
    saved = saved_acts.reshape(NY, NZ, NC * cap, 2, ff)
    pre, down, router = pl.pallas_call(
        functools.partial(kernel, nx, cap),
        out_shape=[
            jax.ShapeDtypeStruct(saved.shape, BF16),
            jax.ShapeDtypeStruct((ff, width), BF16),
            jax.ShapeDtypeStruct((2, tokens), F32),
        ],
        in_specs=[vmem] * 4 + [hbm] * 2 + [vmem] * len(consts),
        out_specs=[hbm, hbm, vmem],
        scratch_shapes=[
            pltpu.VMEM((nx, HALVES, tokens, half), BF16),
            pltpu.VMEM((HALVES, nx, tokens, half), BF16),
            pltpu.VMEM((ne, tokens), BF16),
            pltpu.VMEM((nx, ne, tokens), BF16),
            pltpu.VMEM((ne, HALVES * nx * tokens), F32),
            pltpu.VMEM((NZ, gs * mr, half), BF16),
            pltpu.VMEM((NZ, gs * mr, half), BF16),
            pltpu.VMEM((NZ * nx * own, width), BF16),
            pltpu.VMEM((ff, width), BF16),
            pltpu.VMEM((NZ, NY, NC * cap, 2, ff), BF16),
            pltpu.VMEM((NZ, NY, NC * cap, 2, ff), BF16),
            pltpu.VMEM((ne, 1, 128), F32),
            pltpu.VMEM((ne, 1, 128), F32),
            pltpu.VMEM((NZ, own, 128), F32),
            pltpu.VMEM((NZ, own, ff), BF16),
            pltpu.VMEM((NZ, nx, own, ff), BF16),
            pltpu.VMEM((ff, NZ * nx * own), BF16),
            pltpu.VMEM((2, nx * own, ff), F32),
            pltpu.VMEM((NZ, nx * own, ff), BF16),
            pltpu.VMEM((NZ, nx, own, ff), BF16),
            pltpu.VMEM((NZ, 1, 128), F32),
            pltpu.VMEM((ne, 1, 128), F32),
            pltpu.VMEM((ff, width), F32),
            pltpu.VMEM((ff, width), BF16),
            dma((3,)),
            dma((len(CUTS), nx - 1)), dma((len(CUTS),)),
            dma((nx - 1,)), dma,
            dma((NZ,)), dma((NZ,)), dma,
            dma, dma,
            dma((nx - 1,)), dma, dma,
            dma((NZ,)), dma((NZ,)),
            dma, dma,
            dma((NZ,)), dma((width // 256,)),
        ],
        compiler_params=pltpu.CompilerParams(
            collective_id=0, has_side_effects=True, vmem_limit_bytes=60 << 20
        ),
    )(grad_out, grad_exponent.T, expert_ids.T, combine.T, saved, w_down[0], *consts)
    pieces = 16
    pre, down, router = pl.pallas_call(
        functools.partial(hand_over, pieces),
        out_shape=[jax.ShapeDtypeStruct(v.shape, v.dtype) for v in (pre, down, router)],
        in_specs=[hbm, hbm, vmem],
        out_specs=[hbm, hbm, vmem],
        scratch_shapes=[
            pltpu.VMEM(pre.shape, BF16), pltpu.VMEM(down.shape, BF16), dma((pieces + NY * NZ,)), dma((pieces + NY * NZ,)),
        ],
    )(pre, down, router)
    return pre.reshape(saved_acts.shape), down[None], router.T


def solution(mesh):
    placed = (
        P(("expert", "etp"), None),
        P(("expert", "etp"), None),
        P(("expert", "etp"), None),
        P(("expert", "etp"), None),
        P("expert", "etp", None, None, None, None),
        P("expert", None, "etp"),
    )
    return jax.shard_map(
        local,
        mesh=mesh,
        in_specs=placed,
        out_specs=(
            P("expert", "etp", None, None, None, None),
            P("expert", None, "etp"),
            P(("expert", "etp"), None),
        ),
        check_vma=False,
    )
```

```python
import functools

import jax
import jax.numpy as jnp
import numpy as np
from jax import lax
from jax.experimental import pallas as pl
from jax.experimental.pallas import tpu as pltpu
from jax.sharding import PartitionSpec as P

MESH = pl.DeviceIdType.MESH
F32, BF16, I32 = jnp.float32, jnp.bfloat16, jnp.int32
NY, NZ, NC = 4, 8, 2
HALVES = 2
CUTS = (0, 128, 384)


def power_of_two(exponent):
    return jnp.where(
        exponent <= -2, 0.25, jnp.where(exponent == -1, 0.5, jnp.where(exponent == 0, 1.0, 2.0))
    ).astype(F32)


def matmul(a, b):
    return jnp.dot(a, b, preferred_element_type=F32)


def constants(nx, cap, tok):
    gs = NY * NC
    rc = nx * cap
    own = gs * cap
    order = np.zeros((HALVES, gs * rc, gs * HALVES * rc), np.float32)
    for h in range(HALVES):
        for r in range(nx):
            for i in range(gs):
                for c in range(cap):
                    order[h, r * own + i * cap + c, (i * HALVES + h) * rc + r * cap + c] = 1
    split = np.zeros((2 * own, 2 * own), np.float32)
    for g in range(2):
        for j in range(own):
            split[g * own + j, 2 * j + g] = 1
    repeat = np.zeros((own, gs), np.float32)
    for j in range(own):
        repeat[j, j // cap] = 1
    pick = np.zeros((own, 128), np.float32)
    diag = np.zeros((own, 128), np.float32)
    for j in range(own):
        pick[j, j % cap] = 1
        diag[j, j] = 1
    before = np.triu(np.ones((tok, tok), np.float32), 1)
    bf = lambda a: jnp.asarray(a, BF16)
    return bf(order), bf(split), bf(split.T), bf(repeat), jnp.asarray(pick), jnp.asarray(diag), bf(before)


def kernel(
    nx, cap,
    grad_ref, exp_ref, ids_ref, comb_ref, saved_hbm, w_hbm,
    order_ref, split_ref, join_ref, repeat_ref, pick_ref, diag_ref, before_ref,
    pre_hbm, down_hbm, router_ref,
    xs, tok, tok_near, ksend, krecv, k_near, keys, sbuf, rbuf, rows, w, sv, pstage, wsend, wrecv, wcol,
    scaled, scaled_all, scaled_t, pf, psend, precv, rrow, rrecv, acc, down,
    in_sem, x_ssem, x_rsem, k_ssem, k_rsem, n_ssem, n_rsem, kn_ssem, kn_rsem, d_ssem, d_rsem, d_lsem, w_ssem, w_rsem,
    g_ssem, g_rsem, g_lsem, p_ssem, p_rsem, r_ssem, r_rsem, o_sem, o2_sem,
):
    me = lax.axis_index("expert")
    q = lax.axis_index("etp")
    y, z, core = me // (NZ * NC), (me // NC) % NZ, me % NC
    gs = NY * NC
    rc = nx * cap
    mr = HALVES * rc
    own = gs * cap
    ne = NY * NZ * NC
    tokens = grad_ref.shape[0]
    width = w.shape[1]
    half = width // HALVES
    blocks = exp_ref.shape[0]

    def expert_of(dy, dz, dc):
        return ((y + dy) % NY) * (NZ * NC) + ((z + dz) % NZ) * NC + (core + dc) % NC

    def remote(src, dst, ssem, rsem, e, x):
        return pltpu.make_async_remote_copy(
            src_ref=src, dst_ref=dst, send_sem=ssem, recv_sem=rsem, device_id=(e, x), device_id_type=MESH
        )

    def step_of(k, j):
        paired = (k + NZ - 2) // NZ
        far = (1 + ((k + NZ - 2) % NZ) // 2) * (1 - 2 * (j // 2))
        dz = (1 - paired) * (NZ // 2) * k + paired * (NZ // 2 + far)
        dy = (1 - paired) * j + paired * (2 * (k % 2) + j % 2)
        return dy, (dz + NZ) % NZ

    def source(k, j):
        dy, dz = step_of(k, j)
        return (y - dy + NY) % NY, (z - dz + NZ) % NZ

    w_in = pltpu.make_async_copy(w_hbm, w, in_sem.at[0])
    w_in.start()

    def load_saved(n, _):
        sy, sz = source(n // NY, n % NY)
        pltpu.make_async_copy(saved_hbm.at[sy, sz], sv.at[n // NY, n % NY], in_sem.at[1]).start()
        return 0


    bar = pltpu.get_barrier_semaphore()
    for d in range(1, nx):
        pl.semaphore_signal(bar, inc=1, device_id=(me, (q + d) % nx), device_id_type=MESH)

    def greet(k, _):
        pl.semaphore_signal(bar, inc=1, device_id=((me + k) % ne, q), device_id_type=MESH)
        return 0

    lax.fori_loop(1, ne, greet, 0)

    expert_iota = lax.broadcasted_iota(I32, (ne, tokens), 0)
    a = [jnp.where(expert_iota == ids_ref[k : k + 1, :], 1.0, 0.0) for k in range(2)]
    assigned = a[0] + a[1]
    slot = matmul(assigned.astype(BF16), before_ref[...])
    slot = jnp.where(assigned > 0, slot, -1.0)
    ksend[...] = slot.astype(BF16)
    combine = comb_ref[...].astype(F32)
    weight = a[0] * combine[0:1, :] + a[1] * combine[1:2, :]
    lane = lax.broadcasted_iota(I32, (ne, 128), 1)
    slot_weight = jnp.zeros((ne, 128), F32)
    for c in range(cap):
        total = jnp.sum(jnp.where(slot == c, weight, 0.0), axis=1, keepdims=True)
        slot_weight = jnp.where(lane == c, total, slot_weight)
    wsend[...] = slot_weight.reshape(ne, 1, 128)

    scale_t = power_of_two(exp_ref[...]).astype(BF16)
    blk = width // (width * nx // blocks)
    qb = width // blk
    block_iota = lax.broadcasted_iota(I32, (blocks, width), 0)
    col_block = lax.broadcasted_iota(I32, (blocks, width), 1) // qb
    for j in range(nx):
        expand = jnp.where(block_iota == col_block + j * blk, 1.0, 0.0).astype(BF16)
        scale = lax.dot_general(scale_t, expand, (((0,), (0,)), ((), ())), preferred_element_type=F32)
        deq = (grad_ref[:, j * width : (j + 1) * width].astype(F32) * scale).astype(BF16)
        for h in range(HALVES):
            xs[j, h] = deq[:, h * half : (h + 1) * half]

    pl.semaphore_wait(bar, ne - 1 + nx - 1)

    k_out, x_out = [], []
    for d in range(1, nx):
        p = (q + d) % nx
        k_out.append(remote(ksend, krecv.at[q], k_ssem.at[d - 1], k_rsem, me, p))
        k_out[-1].start()
    cuts = [slice(lo, hi) for lo, hi in zip(CUTS, CUTS[1:] + (half,))]
    for part, cut in enumerate(cuts):
        for d in range(1, nx):
            p = (q + d) % nx
            x_out.append(
                remote(xs.at[p, :, :, cut], tok.at[:, q, :, cut], x_ssem.at[part, d - 1], x_rsem.at[part], me, p)
            )
            x_out[-1].start()
    x_own = pltpu.make_async_copy(xs.at[q], tok.at[:, q], in_sem.at[2])
    x_own.start()
    krecv[q] = ksend[...]
    lax.fori_loop(0, NZ * NY, load_saved, 0)

    def send_weight(k, _):
        group, j, dc = k // gs, (k % gs) // NC, k % NC
        dy, dz = step_of(group, j)
        e = expert_of(dy, dz, dc)
        remote(wsend.at[e], wrecv.at[group * gs + j * NC + core], w_ssem, w_rsem, e, q).start()
        return 0


    remote(krecv.at[pl.ds(0, nx - 1)], krecv.at[pl.ds(0, nx - 1)], k_ssem.at[0], k_rsem, me, (q + 1) % nx).wait_recv()
    near = [((z + NZ - 1) % NZ, (z + 1) % NZ), ((z + 1) % NZ, (z + NZ - 1) % NZ)]

    def device_at(plane):
        return (y * NZ + plane) * NC + core

    kn_out = [
        remote(krecv, k_near.at[i], kn_ssem.at[i], kn_rsem.at[i], device_at(near[i][0]), q) for i in range(2)
    ]
    for c in kn_out:
        c.start()

    def make_keys(i, tables):
        for r in range(nx):
            s = tables[r].astype(F32)
            for h in range(HALVES):
                at = (h * nx + r) * tokens
                keys[i, :, at : at + tokens] = jnp.where(s >= 0, s + (h * rc + r * cap), -1.0)

    make_keys(2, krecv)
    x_own.wait()

    row_iota = lax.broadcasted_iota(I32, (mr, HALVES * nx * tokens), 0).astype(F32)

    def build(k, j, cut, held, i, plane):
        dy, dz = step_of(k, j)
        for c in range(NC):
            e = (((y + dy) % NY) * NZ + (plane + dz) % NZ) * NC + c
            hot = jnp.where(row_iota == keys[i, pl.ds(e, 1), :], 1.0, 0.0).astype(BF16)
            out = matmul(hot, held.reshape(HALVES * nx * tokens, cut.stop - cut.start))
            at = (j * NC + c) * mr
            sbuf[k, at : at + mr, cut] = out.astype(BF16)

    def ends(k, j, dc, cut):
        to, at = j * NC + (core + dc) % NC, j * NC + core
        return (
            sbuf.at[k, pl.ds(pl.multiple_of(to * mr, mr), mr), cut],
            rbuf.at[k, pl.ds(pl.multiple_of(at * mr, mr), mr), cut],
        )

    def send(k, j, dc, cut, plane):
        dy, dz = step_of(k, j)
        e = (((y + dy) % NY) * NZ + (plane + dz) % NZ) * NC + (core + dc) % NC
        src, dst = ends(k, j, dc, cut)
        remote(src, dst, d_ssem.at[k], d_rsem.at[k], e, q).start()

    def dispatch_own(part):
        cut = cuts[part]
        for j in range(NY):
            build(0, j, cut, tok[:, :, :, cut], 2, z)
        for j in range(NY):
            for dc in range(NC):
                if (j, dc) == (0, 0):
                    src, dst = ends(0, 0, 0, cut)
                    pltpu.make_async_copy(src, dst, d_lsem.at[0]).start()
                else:
                    send(0, j, dc, cut, z)

    def dispatch(part, g, _):
        cut = cuts[part]
        later, last = (g + NZ - 2) // (NZ - 1), (g + NZ - 4) // (NZ - 1)
        k = 1 + later * (1 - last) * (g + NZ - 4) + last * (g - 2)
        for j in range(NY):
            i = j // 2
            build(k, j, cut, tok_near[i, :, :, :, cut], i, near[i][1])
        for j in range(NY):
            plane = near[j // 2][1]
            for dc in range(NC):
                if (j % 2, dc) == (0, 0):
                    @pl.when(k != NZ - 2)
                    def _():
                        send(k, j, 0, cut, plane)

                    @pl.when(k == NZ - 2)
                    def _():
                        src, dst = ends(k, j, 0, cut)
                        pltpu.make_async_copy(src, dst, d_lsem.at[1]).start()
                else:
                    send(k, j, dc, cut, plane)
        return 0

    n_out = []

    def pass_on(part):
        cut = cuts[part]
        landed = tok.at[:, pl.ds(0, nx - 1), :, cut]
        remote(landed, landed, x_ssem.at[part, 0], x_rsem.at[part], me, (q + 1) % nx).wait_recv()
        for i in range(2):
            n_out.append(
                remote(
                    tok.at[:, :, :, cut], tok_near.at[i, :, :, :, cut],
                    n_ssem.at[part, i], n_rsem.at[part, i], device_at(near[i][0]), q,
                )
            )
            n_out[-1].start()

    def await_near(part):
        for i in range(2):
            landed = tok_near.at[i, :, :, :, cuts[part]]
            remote(landed, landed, n_ssem.at[part, i], n_rsem.at[part, i], me, (q + 1) % nx).wait_recv()

    def forward(part):
        lax.fori_loop(0, NZ - 1, functools.partial(dispatch, part), 0)

    pass_on(0)
    dispatch_own(0)
    for i in range(2):
        remote(k_near.at[i], k_near.at[i], kn_ssem.at[i], kn_rsem.at[i], me, (q + 1) % nx).wait_recv()
        make_keys(i, k_near.at[i])
    pass_on(1)
    await_near(0)
    forward(0)
    lax.fori_loop(1, ne, send_weight, 0)
    wrecv[core] = wsend[me]
    pass_on(2)
    dispatch_own(1)
    await_near(1)
    forward(1)
    dispatch_own(2)

    pltpu.make_async_copy(sv, sv, in_sem.at[1]).wait()
    remote(wrecv.at[pl.ds(0, ne - 1)], wrecv.at[pl.ds(0, ne - 1)], w_ssem, w_rsem, me, (q + 1) % nx).wait_recv()

    def gate_up(k):
        v = sv[k].reshape(2 * own, w.shape[0])
        gu = matmul(split_ref[...], v)
        gate, up = gu[:own], gu[own:]
        sg = jax.nn.sigmoid(gate)
        return gate, up, sg, gate * sg

    def scale_hidden(g, _):
        gate, up, sg, silu = gate_up(g)
        wr = wrecv[pl.ds(g * gs, gs)].reshape(gs, 128)
        col = jnp.sum(matmul(repeat_ref[...], wr.astype(BF16)) * pick_ref[...], axis=1, keepdims=True)
        wcol[g] = jnp.broadcast_to(col, (own, 128))
        scaled[g] = (col * (silu * up)).astype(BF16)
        return 0

    lax.fori_loop(0, NZ, scale_hidden, 0)
    g_out = []
    for d in range(1, nx):
        g_out.append(remote(scaled, scaled_all.at[:, q], g_ssem.at[d - 1], g_rsem, me, (q + d) % nx))
        g_out[-1].start()
    g_own = pltpu.make_async_copy(scaled, scaled_all.at[:, q], g_lsem)
    g_own.start()
    await_near(2)
    forward(2)
    w_in.wait()

    ff = w.shape[0]
    step = 256

    def turn_scaled():
        remote(scaled_all.at[:, pl.ds(0, nx - 1)], scaled_all.at[:, pl.ds(0, nx - 1)], g_ssem.at[0], g_rsem, me, (q + 1) % nx).wait_recv()
        g_own.wait()
        flat_scaled = scaled_all.reshape(NZ * nx * own, ff)

        def turn(k, _):
            at = pl.multiple_of(k * step, step)
            scaled_t[:, pl.ds(at, step)] = flat_scaled[pl.ds(at, step), :].T
            return 0

        lax.fori_loop(0, NZ * nx * own // step, turn, 0)

    grp = nx * own
    taken = [0, 6, 7, 1, 2, 3, 4, 5]
    stay = [1] + [0] * (NZ - 3) + [2, 0]

    def finish(g):
        landed = precv.at[g, pl.ds(0, nx - 1)]
        remote(landed, landed, p_ssem.at[g], p_rsem.at[g], me, (q + 1) % nx).wait_recv()
        raw = pf[taken.index(g) % 2, pl.ds(pl.multiple_of(q * own, own), own), :]
        for d in range(1, nx):
            raw = raw + precv[g, (q + d) % nx].astype(F32)
        gate, up, sg, silu = gate_up(g)
        part = jnp.sum(silu * up * raw, axis=1, keepdims=True)
        rrow[g] = jnp.sum(part * diag_ref[...], axis=0, keepdims=True)
        for j in range(NY):
            sy, sz = source(g, j)
            for dc in range(NC):
                if (g, j, dc) == (0, 0, 0):
                    rrecv[me] = rrow[g]
                else:
                    e = (sy * NZ + sz) * NC + (core + dc) % NC
                    remote(rrow.at[g], rrecv.at[me], r_ssem, r_rsem, e, q).start()
        hg = wcol[g][:, 0:1] * raw
        g_gate = hg * up * (sg * (1.0 + gate * (1.0 - sg)))
        g_up = hg * silu
        both = jnp.concatenate([g_gate, g_up], axis=0).astype(BF16)
        pstage[g] = matmul(join_ref[...], both).astype(BF16).reshape(pstage.shape[1:])
        for j in range(NY):
            sy, sz = source(g, j)
            pltpu.make_async_copy(pstage.at[g, j], pre_hbm.at[sy, sz], o_sem.at[g]).start()

    def arrive(g):
        part = rbuf.at[g, pl.ds(0, (gs - stay[g]) * mr)]
        remote(part, part, d_ssem.at[g], d_rsem.at[g], me, (q + 1) % nx).wait_recv()
        if stay[g]:
            block = rbuf.at[g, pl.ds(0, stay[g] * mr)]
            pltpu.make_async_copy(block, block, d_lsem.at[stay[g] - 1]).wait()
        at = g * grp
        for h in range(HALVES):
            rows[at : at + grp, h * half : (h + 1) * half] = matmul(order_ref[h], rbuf[g]).astype(BF16)
        part = lax.dot_general(
            rows[at : at + grp, :], w[...], (((1,), (1,)), ((), ())), preferred_element_type=F32
        )
        pf[taken.index(g) % 2] = part
        psend[g] = part.astype(BF16)
        for d in range(1, nx):
            p = (q + d) % nx
            remote(
                psend.at[g, pl.ds(pl.multiple_of(p * own, own), own)], precv.at[g, q],
                p_ssem.at[g], p_rsem.at[g], me, p,
            ).start()

    def product(lo, hi, first, last):
        def tile(k, _):
            at = pl.ds(pl.multiple_of(k * step, step), step)
            total = matmul(scaled_t[:, lo * grp : hi * grp], rows[lo * grp : hi * grp, at])
            if not first:
                total = total + acc[:, at]
            if last:
                down[:, at] = total.astype(BF16)
                pltpu.make_async_copy(down.at[:, at], down_hbm.at[:, at], o2_sem.at[k]).start()
            else:
                acc[:, at] = total
            return 0

        lax.fori_loop(0, width // step, tile, 0)

    arrive(0)
    arrive(6)
    finish(0)
    arrive(7)
    finish(6)
    turn_scaled()
    product(6, 8, True, False)
    finish(7)
    arrive(1)
    product(0, 2, False, False)
    arrive(2)
    finish(1)
    arrive(3)
    finish(2)
    product(2, 4, False, False)
    arrive(4)
    finish(3)
    arrive(5)
    finish(4)
    product(4, 6, False, True)
    finish(5)

    remote(rrecv.at[pl.ds(0, ne - 1)], rrecv.at[pl.ds(0, ne - 1)], r_ssem, r_rsem, me, (q + 1) % nx).wait_recv()
    back = rrecv[...].reshape(ne, 128)
    value = jnp.zeros((ne, tokens), F32)
    slot = ksend[...].astype(F32)
    expert = lax.broadcasted_iota(I32, (ne, 128), 0)
    dy = (expert // (NZ * NC) - y + NY) % NY
    dz = ((expert // NC) % NZ - z + NZ) % NZ
    j = jnp.where(dz % (NZ // 2) == 0, dy, dy % 2 + jnp.where(dz < NZ // 2, 2, 0))
    place = (j * NC + core) * cap
    for c in range(cap):
        column = jnp.sum(jnp.where(lane == place + c, back, 0.0), axis=1, keepdims=True)
        value = jnp.where(slot == c, column, value)
    for k in range(2):
        mine = jnp.where(expert_iota == ids_ref[k : k + 1, :], value, 0.0)
        router_ref[k : k + 1, :] = jnp.sum(mine, axis=0, keepdims=True)

    for c in k_out + kn_out + x_out + n_out + g_out:
        c.wait_send()
    part = wsend.at[pl.ds(0, ne - 1)]
    remote(part, part, w_ssem, w_rsem, me, (q + 1) % nx).wait_send()
    part = rrecv.at[pl.ds(0, ne - 1)]
    remote(part, part, r_ssem, r_rsem, me, (q + 1) % nx).wait_send()
    for j in range(NZ):
        part = sbuf.at[j, pl.ds(0, (gs - stay[j]) * mr)]
        remote(part, part, d_ssem.at[j], d_rsem.at[j], me, (q + 1) % nx).wait_send()
        part = psend.at[j, pl.ds(0, (nx - 1) * own)]
        remote(part, part, p_ssem.at[j], p_rsem.at[j], me, (q + 1) % nx).wait_send()
        pltpu.make_async_copy(pstage.at[j], pre_hbm.at[:, j], o_sem.at[j]).wait()
    for k in range(width // step):
        pltpu.make_async_copy(
            down.at[:, k * step : (k + 1) * step], down_hbm.at[:, k * step : (k + 1) * step], o2_sem.at[k]
        ).wait()


def hand_over(pieces, pre_in, down_in, router_in, pre_out, down_out, router_out, pre_buf, down_buf, in_sem, out_sem):
    parts = []
    rows = down_buf.shape[0] // pieces
    for j in range(pieces):
        at = pl.ds(j * rows, rows)
        parts.append((down_in.at[at], down_buf.at[at], down_out.at[at]))
    for j in range(pre_buf.shape[0]):
        for i in range(pre_buf.shape[1]):
            parts.append((pre_in.at[j, i], pre_buf.at[j, i], pre_out.at[j, i]))
    loads = [pltpu.make_async_copy(a, b, in_sem.at[n]) for n, (a, b, _) in enumerate(parts)]
    stores = [pltpu.make_async_copy(b, c, out_sem.at[n]) for n, (_, b, c) in enumerate(parts)]
    for c in loads:
        c.start()
    router_out[...] = router_in[...]
    for load, store in zip(loads, stores):
        load.wait()
        store.start()
    for c in stores:
        c.wait()


def local(grad_out, grad_exponent, expert_ids, combine, saved_acts, w_down):
    nx = lax.axis_size("etp")
    ne = NY * NZ * NC
    tokens, features = grad_out.shape
    cap, ff = saved_acts.shape[3], saved_acts.shape[5]
    width = features // nx
    half = width // HALVES
    gs = NY * NC
    own = gs * cap
    mr = HALVES * nx * cap
    consts = constants(nx, cap, tokens)
    vmem = pl.BlockSpec(memory_space=pltpu.VMEM)
    hbm = pl.BlockSpec(memory_space=pl.ANY)
    dma = pltpu.SemaphoreType.DMA
    saved = saved_acts.reshape(NY, NZ, NC * cap, 2, ff)
    pre, down, router = pl.pallas_call(
        functools.partial(kernel, nx, cap),
        out_shape=[
            jax.ShapeDtypeStruct(saved.shape, BF16),
            jax.ShapeDtypeStruct((ff, width), BF16),
            jax.ShapeDtypeStruct((2, tokens), F32),
        ],
        in_specs=[vmem] * 4 + [hbm] * 2 + [vmem] * len(consts),
        out_specs=[hbm, hbm, vmem],
        scratch_shapes=[
            pltpu.VMEM((nx, HALVES, tokens, half), BF16),
            pltpu.VMEM((HALVES, nx, tokens, half), BF16),
            pltpu.VMEM((2, HALVES, nx, tokens, half), BF16),
            pltpu.VMEM((ne, tokens), BF16),
            pltpu.VMEM((nx, ne, tokens), BF16),
            pltpu.VMEM((2, nx, ne, tokens), BF16),
            pltpu.VMEM((3, ne, HALVES * nx * tokens), F32),
            pltpu.VMEM((NZ, gs * mr, half), BF16),
            pltpu.VMEM((NZ, gs * mr, half), BF16),
            pltpu.VMEM((NZ * nx * own, width), BF16),
            pltpu.VMEM((ff, width), BF16),
            pltpu.VMEM((NZ, NY, NC * cap, 2, ff), BF16),
            pltpu.VMEM((NZ, NY, NC * cap, 2, ff), BF16),
            pltpu.VMEM((ne, 1, 128), F32),
            pltpu.VMEM((ne, 1, 128), F32),
            pltpu.VMEM((NZ, own, 128), F32),
            pltpu.VMEM((NZ, own, ff), BF16),
            pltpu.VMEM((NZ, nx, own, ff), BF16),
            pltpu.VMEM((ff, NZ * nx * own), BF16),
            pltpu.VMEM((2, nx * own, ff), F32),
            pltpu.VMEM((NZ, nx * own, ff), BF16),
            pltpu.VMEM((NZ, nx, own, ff), BF16),
            pltpu.VMEM((NZ, 1, 128), F32),
            pltpu.VMEM((ne, 1, 128), F32),
            pltpu.VMEM((ff, width), F32),
            pltpu.VMEM((ff, width), BF16),
            dma((3,)),
            dma((len(CUTS), nx - 1)), dma((len(CUTS),)),
            dma((nx - 1,)), dma,
            dma((len(CUTS), 2)), dma((len(CUTS), 2)),
            dma((2,)), dma((2,)),
            dma((NZ,)), dma((NZ,)), dma((2,)),
            dma, dma,
            dma((nx - 1,)), dma, dma,
            dma((NZ,)), dma((NZ,)),
            dma, dma,
            dma((NZ,)), dma((width // 256,)),
        ],
        compiler_params=pltpu.CompilerParams(
            collective_id=0, has_side_effects=True, vmem_limit_bytes=60 << 20
        ),
    )(grad_out, grad_exponent.T, expert_ids.T, combine.T, saved, w_down[0], *consts)
    pieces = 16
    pre, down, router = pl.pallas_call(
        functools.partial(hand_over, pieces),
        out_shape=[jax.ShapeDtypeStruct(v.shape, v.dtype) for v in (pre, down, router)],
        in_specs=[hbm, hbm, vmem],
        out_specs=[hbm, hbm, vmem],
        scratch_shapes=[
            pltpu.VMEM(pre.shape, BF16), pltpu.VMEM(down.shape, BF16), dma((pieces + NY * NZ,)), dma((pieces + NY * NZ,)),
        ],
    )(pre, down, router)
    return pre.reshape(saved_acts.shape), down[None], router.T


def solution(mesh):
    placed = (
        P(("expert", "etp"), None),
        P(("expert", "etp"), None),
        P(("expert", "etp"), None),
        P(("expert", "etp"), None),
        P("expert", "etp", None, None, None, None),
        P("expert", None, "etp"),
    )
    return jax.shard_map(
        local,
        mesh=mesh,
        in_specs=placed,
        out_specs=(
            P("expert", "etp", None, None, None, None),
            P("expert", None, "etp"),
            P(("expert", "etp"), None),
        ),
        check_vma=False,
    )
```

```python
import functools

import jax
import jax.numpy as jnp
import numpy as np
from jax import lax
from jax.experimental import pallas as pl
from jax.experimental.pallas import tpu as pltpu
from jax.sharding import PartitionSpec as P

MESH = pl.DeviceIdType.MESH
F32, BF16, I32 = jnp.float32, jnp.bfloat16, jnp.int32
NY, NZ, NC = 4, 8, 2
HALVES = 2
CUTS = (0, 128, 384)


def power_of_two(exponent):
    return jnp.where(
        exponent <= -2, 0.25, jnp.where(exponent == -1, 0.5, jnp.where(exponent == 0, 1.0, 2.0))
    ).astype(F32)


def matmul(a, b):
    return jnp.dot(a, b, preferred_element_type=F32)


def constants(nx, cap, tok):
    gs = NY * NC
    rc = nx * cap
    own = gs * cap
    order = np.zeros((HALVES, gs * rc, gs * HALVES * rc), np.float32)
    for h in range(HALVES):
        for r in range(nx):
            for i in range(gs):
                for c in range(cap):
                    order[h, r * own + i * cap + c, (i * HALVES + h) * rc + r * cap + c] = 1
    split = np.zeros((2 * own, 2 * own), np.float32)
    for g in range(2):
        for j in range(own):
            split[g * own + j, 2 * j + g] = 1
    repeat = np.zeros((own, gs), np.float32)
    for j in range(own):
        repeat[j, j // cap] = 1
    pick = np.zeros((own, 128), np.float32)
    diag = np.zeros((own, 128), np.float32)
    for j in range(own):
        pick[j, j % cap] = 1
        diag[j, j] = 1
    before = np.triu(np.ones((tok, tok), np.float32), 1)
    bf = lambda a: jnp.asarray(a, BF16)
    return bf(order), bf(split), bf(split.T), bf(repeat), jnp.asarray(pick), jnp.asarray(diag), bf(before)


def kernel(
    nx, cap,
    grad_ref, exp_ref, ids_ref, comb_ref, saved_hbm, w_hbm,
    order_ref, split_ref, join_ref, repeat_ref, pick_ref, diag_ref, before_ref,
    pre_hbm, down_hbm, router_ref,
    xs, tok, tok_near, ksend, krecv, k_near, keys, sbuf, rbuf, rows, w, sv, pstage, wsend, wrecv, wcol,
    scaled, scaled_all, scaled_t, pf, psend, precv, rrow, rrecv, acc, down,
    in_sem, x_ssem, x_rsem, k_ssem, k_rsem, n_ssem, n_rsem, kn_ssem, kn_rsem, d_ssem, d_rsem, d_lsem, w_ssem, w_rsem,
    g_ssem, g_rsem, g_lsem, p_ssem, p_rsem, r_ssem, r_rsem, o_sem, o2_sem,
):
    me = lax.axis_index("expert")
    q = lax.axis_index("etp")
    y, z, core = me // (NZ * NC), (me // NC) % NZ, me % NC
    gs = NY * NC
    rc = nx * cap
    mr = HALVES * rc
    own = gs * cap
    ne = NY * NZ * NC
    tokens = grad_ref.shape[0]
    width = w.shape[1]
    half = width // HALVES
    blocks = exp_ref.shape[0]

    def expert_of(dy, dz, dc):
        return ((y + dy) % NY) * (NZ * NC) + ((z + dz) % NZ) * NC + (core + dc) % NC

    def remote(src, dst, ssem, rsem, e, x):
        return pltpu.make_async_remote_copy(
            src_ref=src, dst_ref=dst, send_sem=ssem, recv_sem=rsem, device_id=(e, x), device_id_type=MESH
        )

    def step_of(k, j):
        paired = (k + NZ - 2) // NZ
        far = (1 + ((k + NZ - 2) % NZ) // 2) * (1 - 2 * (j // 2))
        dz = (1 - paired) * (NZ // 2) * k + paired * (NZ // 2 + far)
        dy = (1 - paired) * j + paired * (2 * (k % 2) + j % 2)
        return dy, (dz + NZ) % NZ

    def source(k, j):
        dy, dz = step_of(k, j)
        return (y - dy + NY) % NY, (z - dz + NZ) % NZ

    w_in = pltpu.make_async_copy(w_hbm, w, in_sem.at[0])
    w_in.start()

    def load_saved(n, _):
        sy, sz = source(n // NY, n % NY)
        pltpu.make_async_copy(saved_hbm.at[sy, sz], sv.at[n // NY, n % NY], in_sem.at[1]).start()
        return 0


    bar = pltpu.get_barrier_semaphore()
    for d in range(1, nx):
        pl.semaphore_signal(bar, inc=1, device_id=(me, (q + d) % nx), device_id_type=MESH)

    def greet(k, _):
        pl.semaphore_signal(bar, inc=1, device_id=((me + k) % ne, q), device_id_type=MESH)
        return 0

    lax.fori_loop(1, ne, greet, 0)

    expert_iota = lax.broadcasted_iota(I32, (ne, tokens), 0)
    a = [jnp.where(expert_iota == ids_ref[k : k + 1, :], 1.0, 0.0) for k in range(2)]
    assigned = a[0] + a[1]
    slot = matmul(assigned.astype(BF16), before_ref[...])
    slot = jnp.where(assigned > 0, slot, -1.0)
    ksend[...] = slot.astype(BF16)
    combine = comb_ref[...].astype(F32)
    weight = a[0] * combine[0:1, :] + a[1] * combine[1:2, :]
    lane = lax.broadcasted_iota(I32, (ne, 128), 1)
    slot_weight = jnp.zeros((ne, 128), F32)
    for c in range(cap):
        total = jnp.sum(jnp.where(slot == c, weight, 0.0), axis=1, keepdims=True)
        slot_weight = jnp.where(lane == c, total, slot_weight)
    wsend[...] = slot_weight.reshape(ne, 1, 128)

    scale_t = power_of_two(exp_ref[...]).astype(BF16)
    blk = width // (width * nx // blocks)
    qb = width // blk
    block_iota = lax.broadcasted_iota(I32, (blocks, width), 0)
    col_block = lax.broadcasted_iota(I32, (blocks, width), 1) // qb
    for j in range(nx):
        expand = jnp.where(block_iota == col_block + j * blk, 1.0, 0.0).astype(BF16)
        scale = lax.dot_general(scale_t, expand, (((0,), (0,)), ((), ())), preferred_element_type=F32)
        deq = (grad_ref[:, j * width : (j + 1) * width].astype(F32) * scale).astype(BF16)
        for h in range(HALVES):
            xs[j, h] = deq[:, h * half : (h + 1) * half]

    pl.semaphore_wait(bar, ne - 1 + nx - 1)

    k_out, x_out = [], []
    for d in range(1, nx):
        p = (q + d) % nx
        k_out.append(remote(ksend, krecv.at[q], k_ssem.at[d - 1], k_rsem, me, p))
        k_out[-1].start()
    cuts = [slice(lo, hi) for lo, hi in zip(CUTS, CUTS[1:] + (half,))]
    for part, cut in enumerate(cuts):
        for d in range(1, nx):
            p = (q + d) % nx
            x_out.append(
                remote(xs.at[p, :, :, cut], tok.at[:, q, :, cut], x_ssem.at[part, d - 1], x_rsem.at[part], me, p)
            )
            x_out[-1].start()
    x_own = pltpu.make_async_copy(xs.at[q], tok.at[:, q], in_sem.at[2])
    x_own.start()
    krecv[q] = ksend[...]
    lax.fori_loop(0, NZ * NY, load_saved, 0)

    def send_weight(k, _):
        group, j, dc = k // gs, (k % gs) // NC, k % NC
        dy, dz = step_of(group, j)
        e = expert_of(dy, dz, dc)
        remote(wsend.at[e], wrecv.at[group * gs + j * NC + core], w_ssem, w_rsem, e, q).start()
        return 0


    remote(krecv.at[pl.ds(0, nx - 1)], krecv.at[pl.ds(0, nx - 1)], k_ssem.at[0], k_rsem, me, (q + 1) % nx).wait_recv()
    near = [((z + NZ - 1) % NZ, (z + 1) % NZ), ((z + 1) % NZ, (z + NZ - 1) % NZ)]

    def device_at(plane):
        return (y * NZ + plane) * NC + core

    kn_out = [
        remote(krecv, k_near.at[i], kn_ssem.at[i], kn_rsem.at[i], device_at(near[i][0]), q) for i in range(2)
    ]
    for c in kn_out:
        c.start()

    def make_keys(i, tables):
        for r in range(nx):
            s = tables[r].astype(F32)
            for h in range(HALVES):
                at = (h * nx + r) * tokens
                keys[i, :, at : at + tokens] = jnp.where(s >= 0, s + (h * rc + r * cap), -1.0)

    make_keys(2, krecv)
    x_own.wait()

    row_iota = lax.broadcasted_iota(I32, (mr, HALVES * nx * tokens), 0).astype(F32)

    def build(k, j, cut, held, i, plane):
        dy, dz = step_of(k, j)
        for c in range(NC):
            e = (((y + dy) % NY) * NZ + (plane + dz) % NZ) * NC + c
            hot = jnp.where(row_iota == keys[i, pl.ds(e, 1), :], 1.0, 0.0).astype(BF16)
            out = matmul(hot, held.reshape(HALVES * nx * tokens, cut.stop - cut.start))
            at = (j * NC + c) * mr
            sbuf[k, at : at + mr, cut] = out.astype(BF16)

    def ends(k, j, dc, cut):
        to, at = j * NC + (core + dc) % NC, j * NC + core
        return (
            sbuf.at[k, pl.ds(pl.multiple_of(to * mr, mr), mr), cut],
            rbuf.at[k, pl.ds(pl.multiple_of(at * mr, mr), mr), cut],
        )

    def send(k, j, dc, cut, plane):
        dy, dz = step_of(k, j)
        e = (((y + dy) % NY) * NZ + (plane + dz) % NZ) * NC + (core + dc) % NC
        src, dst = ends(k, j, dc, cut)
        remote(src, dst, d_ssem.at[k], d_rsem.at[k], e, q).start()

    def dispatch_own(part):
        cut = cuts[part]
        for j in range(NY):
            build(0, j, cut, tok[:, :, :, cut], 2, z)
        for j in range(NY):
            for dc in range(NC):
                if (j, dc) == (0, 0):
                    src, dst = ends(0, 0, 0, cut)
                    pltpu.make_async_copy(src, dst, d_lsem.at[0]).start()
                else:
                    send(0, j, dc, cut, z)

    def dispatch(part, g, _):
        cut = cuts[part]
        later, last = (g + NZ - 2) // (NZ - 1), (g + NZ - 4) // (NZ - 1)
        k = 1 + later * (1 - last) * (g + NZ - 4) + last * (g - 2)
        for j in range(NY):
            i = j // 2
            build(k, j, cut, tok_near[i, :, :, :, cut], i, near[i][1])
        for j in range(NY):
            plane = near[j // 2][1]
            for dc in range(NC):
                if (j % 2, dc) == (0, 0):
                    @pl.when(k != NZ - 2)
                    def _():
                        send(k, j, 0, cut, plane)

                    @pl.when(k == NZ - 2)
                    def _():
                        src, dst = ends(k, j, 0, cut)
                        pltpu.make_async_copy(src, dst, d_lsem.at[1]).start()
                else:
                    send(k, j, dc, cut, plane)
        return 0

    n_out = []

    def pass_on(part):
        cut = cuts[part]
        landed = tok.at[:, pl.ds(0, nx - 1), :, cut]
        remote(landed, landed, x_ssem.at[part, 0], x_rsem.at[part], me, (q + 1) % nx).wait_recv()
        for i in range(2):
            n_out.append(
                remote(
                    tok.at[:, :, :, cut], tok_near.at[i, :, :, :, cut],
                    n_ssem.at[part, i], n_rsem.at[part, i], device_at(near[i][0]), q,
                )
            )
            n_out[-1].start()

    def await_near(part):
        for i in range(2):
            landed = tok_near.at[i, :, :, :, cuts[part]]
            remote(landed, landed, n_ssem.at[part, i], n_rsem.at[part, i], me, (q + 1) % nx).wait_recv()

    def forward(part):
        lax.fori_loop(0, NZ - 1, functools.partial(dispatch, part), 0)

    pass_on(0)
    dispatch_own(0)
    for i in range(2):
        remote(k_near.at[i], k_near.at[i], kn_ssem.at[i], kn_rsem.at[i], me, (q + 1) % nx).wait_recv()
        make_keys(i, k_near.at[i])
    pass_on(1)
    await_near(0)
    forward(0)
    lax.fori_loop(1, ne, send_weight, 0)
    wrecv[core] = wsend[me]
    pass_on(2)
    dispatch_own(1)
    await_near(1)
    forward(1)
    dispatch_own(2)

    pltpu.make_async_copy(sv, sv, in_sem.at[1]).wait()
    remote(wrecv.at[pl.ds(0, ne - 1)], wrecv.at[pl.ds(0, ne - 1)], w_ssem, w_rsem, me, (q + 1) % nx).wait_recv()

    def gate_up(k):
        v = sv[k].reshape(2 * own, w.shape[0])
        gu = matmul(split_ref[...], v)
        gate, up = gu[:own], gu[own:]
        sg = jax.nn.sigmoid(gate)
        return gate, up, sg, gate * sg

    def scale_hidden(g, _):
        gate, up, sg, silu = gate_up(g)
        wr = wrecv[pl.ds(g * gs, gs)].reshape(gs, 128)
        col = jnp.sum(matmul(repeat_ref[...], wr.astype(BF16)) * pick_ref[...], axis=1, keepdims=True)
        wcol[g] = jnp.broadcast_to(col, (own, 128))
        scaled[g] = (col * (silu * up)).astype(BF16)
        return 0

    lax.fori_loop(0, NZ, scale_hidden, 0)
    g_out = []
    for d in range(1, nx):
        g_out.append(remote(scaled, scaled_all.at[:, q], g_ssem.at[d - 1], g_rsem, me, (q + d) % nx))
        g_out[-1].start()
    g_own = pltpu.make_async_copy(scaled, scaled_all.at[:, q], g_lsem)
    g_own.start()
    await_near(2)
    forward(2)
    w_in.wait()

    ff = w.shape[0]
    step = 256

    def turn_scaled():
        remote(scaled_all.at[:, pl.ds(0, nx - 1)], scaled_all.at[:, pl.ds(0, nx - 1)], g_ssem.at[0], g_rsem, me, (q + 1) % nx).wait_recv()
        g_own.wait()
        flat_scaled = scaled_all.reshape(NZ * nx * own, ff)

        def turn(k, _):
            at = pl.multiple_of(k * step, step)
            scaled_t[:, pl.ds(at, step)] = flat_scaled[pl.ds(at, step), :].T
            return 0

        lax.fori_loop(0, NZ * nx * own // step, turn, 0)

    grp = nx * own
    taken = [0, 6, 7, 1, 2, 3, 4, 5]
    stay = [1] + [0] * (NZ - 3) + [2, 0]

    def finish(g):
        landed = precv.at[g, pl.ds(0, nx - 1)]
        remote(landed, landed, p_ssem.at[g], p_rsem.at[g], me, (q + 1) % nx).wait_recv()
        raw = pf[taken.index(g) % 2, pl.ds(pl.multiple_of(q * own, own), own), :]
        for d in range(1, nx):
            raw = raw + precv[g, (q + d) % nx].astype(F32)
        gate, up, sg, silu = gate_up(g)
        part = jnp.sum(silu * up * raw, axis=1, keepdims=True)
        rrow[g] = jnp.sum(part * diag_ref[...], axis=0, keepdims=True)
        for j in range(NY):
            sy, sz = source(g, j)
            for dc in range(NC):
                if (g, j, dc) == (0, 0, 0):
                    rrecv[me] = rrow[g]
                else:
                    e = (sy * NZ + sz) * NC + (core + dc) % NC
                    remote(rrow.at[g], rrecv.at[me], r_ssem, r_rsem, e, q).start()
        hg = wcol[g][:, 0:1] * raw
        g_gate = hg * up * (sg * (1.0 + gate * (1.0 - sg)))
        g_up = hg * silu
        both = jnp.concatenate([g_gate, g_up], axis=0).astype(BF16)
        pstage[g] = matmul(join_ref[...], both).astype(BF16).reshape(pstage.shape[1:])
        for j in range(NY):
            sy, sz = source(g, j)
            pltpu.make_async_copy(pstage.at[g, j], pre_hbm.at[sy, sz], o_sem.at[g]).start()

    def arrive(g):
        part = rbuf.at[g, pl.ds(0, (gs - stay[g]) * mr)]
        remote(part, part, d_ssem.at[g], d_rsem.at[g], me, (q + 1) % nx).wait_recv()
        if stay[g]:
            block = rbuf.at[g, pl.ds(0, stay[g] * mr)]
            pltpu.make_async_copy(block, block, d_lsem.at[stay[g] - 1]).wait()
        at = g * grp
        for h in range(HALVES):
            rows[at : at + grp, h * half : (h + 1) * half] = matmul(order_ref[h], rbuf[g]).astype(BF16)
        part = lax.dot_general(
            rows[at : at + grp, :], w[...], (((1,), (1,)), ((), ())), preferred_element_type=F32
        )
        pf[taken.index(g) % 2] = part
        psend[g] = part.astype(BF16)
        for d in range(1, nx):
            p = (q + d) % nx
            remote(
                psend.at[g, pl.ds(pl.multiple_of(p * own, own), own)], precv.at[g, q],
                p_ssem.at[g], p_rsem.at[g], me, p,
            ).start()

    def product(lo, hi, first, last):
        def tile(k, _):
            at = pl.ds(pl.multiple_of(k * step, step), step)
            total = matmul(scaled_t[:, lo * grp : hi * grp], rows[lo * grp : hi * grp, at])
            if not first:
                total = total + acc[:, at]
            if last:
                down[:, at] = total.astype(BF16)
                pltpu.make_async_copy(down.at[:, at], down_hbm.at[:, at], o2_sem.at[k]).start()
            else:
                acc[:, at] = total
            return 0

        lax.fori_loop(0, width // step, tile, 0)

    arrive(0)
    arrive(6)
    finish(0)
    arrive(7)
    finish(6)
    turn_scaled()
    product(6, 8, True, False)
    finish(7)
    arrive(1)
    product(0, 2, False, False)
    arrive(2)
    finish(1)
    arrive(3)
    finish(2)
    arrive(4)
    finish(3)
    arrive(5)
    product(2, 6, False, True)
    finish(4)
    finish(5)

    remote(rrecv.at[pl.ds(0, ne - 1)], rrecv.at[pl.ds(0, ne - 1)], r_ssem, r_rsem, me, (q + 1) % nx).wait_recv()
    back = rrecv[...].reshape(ne, 128)
    value = jnp.zeros((ne, tokens), F32)
    slot = ksend[...].astype(F32)
    expert = lax.broadcasted_iota(I32, (ne, 128), 0)
    dy = (expert // (NZ * NC) - y + NY) % NY
    dz = ((expert // NC) % NZ - z + NZ) % NZ
    j = jnp.where(dz % (NZ // 2) == 0, dy, dy % 2 + jnp.where(dz < NZ // 2, 2, 0))
    place = (j * NC + core) * cap
    for c in range(cap):
        column = jnp.sum(jnp.where(lane == place + c, back, 0.0), axis=1, keepdims=True)
        value = jnp.where(slot == c, column, value)
    for k in range(2):
        mine = jnp.where(expert_iota == ids_ref[k : k + 1, :], value, 0.0)
        router_ref[k : k + 1, :] = jnp.sum(mine, axis=0, keepdims=True)

    for c in k_out + kn_out + x_out + n_out + g_out:
        c.wait_send()
    part = wsend.at[pl.ds(0, ne - 1)]
    remote(part, part, w_ssem, w_rsem, me, (q + 1) % nx).wait_send()
    part = rrecv.at[pl.ds(0, ne - 1)]
    remote(part, part, r_ssem, r_rsem, me, (q + 1) % nx).wait_send()
    for j in range(NZ):
        part = sbuf.at[j, pl.ds(0, (gs - stay[j]) * mr)]
        remote(part, part, d_ssem.at[j], d_rsem.at[j], me, (q + 1) % nx).wait_send()
        part = psend.at[j, pl.ds(0, (nx - 1) * own)]
        remote(part, part, p_ssem.at[j], p_rsem.at[j], me, (q + 1) % nx).wait_send()
        pltpu.make_async_copy(pstage.at[j], pre_hbm.at[:, j], o_sem.at[j]).wait()
    for k in range(width // step):
        pltpu.make_async_copy(
            down.at[:, k * step : (k + 1) * step], down_hbm.at[:, k * step : (k + 1) * step], o2_sem.at[k]
        ).wait()


def hand_over(pieces, pre_in, down_in, router_in, pre_out, down_out, router_out, pre_buf, down_buf, in_sem, out_sem):
    parts = []
    rows = down_buf.shape[0] // pieces
    for j in range(pieces):
        at = pl.ds(j * rows, rows)
        parts.append((down_in.at[at], down_buf.at[at], down_out.at[at]))
    for j in range(pre_buf.shape[0]):
        parts.append((pre_in.at[j], pre_buf.at[j], pre_out.at[j]))
    loads = [pltpu.make_async_copy(a, b, in_sem.at[n]) for n, (a, b, _) in enumerate(parts)]
    stores = [pltpu.make_async_copy(b, c, out_sem.at[n]) for n, (_, b, c) in enumerate(parts)]
    for c in loads:
        c.start()
    router_out[...] = router_in[...]
    for load, store in zip(loads, stores):
        load.wait()
        store.start()
    for c in stores:
        c.wait()


def local(grad_out, grad_exponent, expert_ids, combine, saved_acts, w_down):
    nx = lax.axis_size("etp")
    ne = NY * NZ * NC
    tokens, features = grad_out.shape
    cap, ff = saved_acts.shape[3], saved_acts.shape[5]
    width = features // nx
    half = width // HALVES
    gs = NY * NC
    own = gs * cap
    mr = HALVES * nx * cap
    consts = constants(nx, cap, tokens)
    vmem = pl.BlockSpec(memory_space=pltpu.VMEM)
    hbm = pl.BlockSpec(memory_space=pl.ANY)
    dma = pltpu.SemaphoreType.DMA
    saved = saved_acts.reshape(NY, NZ, NC * cap, 2, ff)
    pre, down, router = pl.pallas_call(
        functools.partial(kernel, nx, cap),
        out_shape=[
            jax.ShapeDtypeStruct(saved.shape, BF16),
            jax.ShapeDtypeStruct((ff, width), BF16),
            jax.ShapeDtypeStruct((2, tokens), F32),
        ],
        in_specs=[vmem] * 4 + [hbm] * 2 + [vmem] * len(consts),
        out_specs=[hbm, hbm, vmem],
        scratch_shapes=[
            pltpu.VMEM((nx, HALVES, tokens, half), BF16),
            pltpu.VMEM((HALVES, nx, tokens, half), BF16),
            pltpu.VMEM((2, HALVES, nx, tokens, half), BF16),
            pltpu.VMEM((ne, tokens), BF16),
            pltpu.VMEM((nx, ne, tokens), BF16),
            pltpu.VMEM((2, nx, ne, tokens), BF16),
            pltpu.VMEM((3, ne, HALVES * nx * tokens), F32),
            pltpu.VMEM((NZ, gs * mr, half), BF16),
            pltpu.VMEM((NZ, gs * mr, half), BF16),
            pltpu.VMEM((NZ * nx * own, width), BF16),
            pltpu.VMEM((ff, width), BF16),
            pltpu.VMEM((NZ, NY, NC * cap, 2, ff), BF16),
            pltpu.VMEM((NZ, NY, NC * cap, 2, ff), BF16),
            pltpu.VMEM((ne, 1, 128), F32),
            pltpu.VMEM((ne, 1, 128), F32),
            pltpu.VMEM((NZ, own, 128), F32),
            pltpu.VMEM((NZ, own, ff), BF16),
            pltpu.VMEM((NZ, nx, own, ff), BF16),
            pltpu.VMEM((ff, NZ * nx * own), BF16),
            pltpu.VMEM((2, nx * own, ff), F32),
            pltpu.VMEM((NZ, nx * own, ff), BF16),
            pltpu.VMEM((NZ, nx, own, ff), BF16),
            pltpu.VMEM((NZ, 1, 128), F32),
            pltpu.VMEM((ne, 1, 128), F32),
            pltpu.VMEM((ff, width), F32),
            pltpu.VMEM((ff, width), BF16),
            dma((3,)),
            dma((len(CUTS), nx - 1)), dma((len(CUTS),)),
            dma((nx - 1,)), dma,
            dma((len(CUTS), 2)), dma((len(CUTS), 2)),
            dma((2,)), dma((2,)),
            dma((NZ,)), dma((NZ,)), dma((2,)),
            dma, dma,
            dma((nx - 1,)), dma, dma,
            dma((NZ,)), dma((NZ,)),
            dma, dma,
            dma((NZ,)), dma((width // 256,)),
        ],
        compiler_params=pltpu.CompilerParams(
            collective_id=0, has_side_effects=True, vmem_limit_bytes=60 << 20
        ),
    )(grad_out, grad_exponent.T, expert_ids.T, combine.T, saved, w_down[0], *consts)
    pieces = 4
    pre, down, router = pl.pallas_call(
        functools.partial(hand_over, pieces),
        out_shape=[jax.ShapeDtypeStruct(v.shape, v.dtype) for v in (pre, down, router)],
        in_specs=[hbm, hbm, vmem],
        out_specs=[hbm, hbm, vmem],
        scratch_shapes=[
            pltpu.VMEM(pre.shape, BF16), pltpu.VMEM(down.shape, BF16), dma((pieces + NY,)), dma((pieces + NY,)),
        ],
    )(pre, down, router)
    return pre.reshape(saved_acts.shape), down[None], router.T


def solution(mesh):
    placed = (
        P(("expert", "etp"), None),
        P(("expert", "etp"), None),
        P(("expert", "etp"), None),
        P(("expert", "etp"), None),
        P("expert", "etp", None, None, None, None),
        P("expert", None, "etp"),
    )
    return jax.shard_map(
        local,
        mesh=mesh,
        in_specs=placed,
        out_specs=(
            P("expert", "etp", None, None, None, None),
            P("expert", None, "etp"),
            P(("expert", "etp"), None),
        ),
        check_vma=False,
    )
```
